512 devices in a mesh: section: 16 (over y, z_hi), dp: 8 (over x, core), mp: 4 (over z_lo).
Axes of the slice: x: 4, y: 4, z: 16 (z_hi: 4, z_lo: 4; z = z_hi * 4 + z_lo), core: 2. Of those that a mesh axis runs over, the one named last changes fastest.
Arguments:
- act_in: bfloat16 [16, 160, 6144], P('section', None, ('dp', 'mp')), may hold values from -6 to 6
- grad_in: bfloat16 [16, 160, 6144], P('section', None, ('dp', 'mp')), may hold values from -6 to 6
- weight: bfloat16 [16, 6144, 6144], P('section', ('dp', 'mp')), may hold values from -0.078125 to 0.078125
- gain: bfloat16 [16, 6144], P('section', ('dp', 'mp')), may hold values from 0.5 to 1.5
- preempted: int32 [16, 160], P('section'), may hold values 0 or 1
Outputs:
- next_input: bfloat16 [16, 160, 6144], P('section', None, ('dp', 'mp'))
- shadow: bfloat16 [16, 160, 6144], P('section', None, ('dp', 'mp'))
- input_grad: bfloat16 [16, 160, 6144], P('section', None, ('dp', 'mp'))
- weight_grad: bfloat16 [16, 6144, 6144], P('section', ('dp', 'mp'))
- gain_grad: float32 [16, 6144], P('section', ('dp', 'mp'))
The draws below stay inside these ranges and needn't reach their ends.
All inputs are finite; a program needn't handle non-finite values. No bound on the sum of `preempted` on one device may be relied on, other than what follows from the above.
Results may differ from the reference program's by a relative error of at most 0.0062.
Values may be sent and summed in bfloat16 or wider, within the bound.
A program may use at most 64 MiB of HBM per device.

```python
import jax
import jax.numpy as jnp
from jax import lax

D = 6144
TOKENS = 160
N_SECTION = 16


def place_ends(result, own_key, smallest, top_value):
    dims = result.shape
    spot = [jax.random.randint(jax.random.fold_in(own_key, axis), (), 0, dims[axis]) for axis in range(len(dims))]
    result = result.at[tuple(spot)].set(smallest)
    longest = dims.index(max(dims))
    spot[longest] = (spot[longest] + 1) % dims[longest]
    return result.at[tuple(spot)].set(top_value)


def shard_levels(key, extent, pieces, smallest, top_value):
    level = 1.0
    for position, shards_of in pieces:
        steps = jax.random.uniform(jax.random.fold_in(jax.random.fold_in(key, 6), position), (shards_of,), jnp.float32, smallest / len(pieces), top_value / len(pieces))
        level = level * jnp.repeat(jnp.exp(steps), extent[position] // shards_of).reshape((-1,) + (1,) * (len(extent) - 1 - position))
    return level


def gaussian(stream_key, shape, spread, most, cuts=(), kind=jnp.bfloat16):
    array = spread * jax.random.normal(stream_key, shape, jnp.float32)
    if cuts:
        array = array * shard_levels(stream_key, shape, cuts, -0.22, 0.18)
    return jnp.clip(array, -most, most).astype(kind)


def setup_inputs(seed: int = 0) -> dict:
    key_list = jax.random.split(jax.random.key(seed), 6)
    act_in = gaussian(key_list[0], (N_SECTION, TOKENS, D), 1.0, 6.0, ((0, 16), (2, 32)))
    grad_in = gaussian(key_list[1], (N_SECTION, TOKENS, D), 1.0, 6.0, ((0, 16), (2, 32)))
    weight = gaussian(key_list[2], (N_SECTION, D, D), D ** -0.5, 0.078125, ((0, 16), (1, 32)))
    gain = jnp.clip(1.0 + 0.1 * jax.random.normal(key_list[3], (N_SECTION, D), jnp.float32), 0.5, 1.5).astype(jnp.bfloat16)
    preempted = place_ends((jax.random.randint(key_list[4], (N_SECTION, TOKENS), 0, 2) < 1).astype(jnp.int32), jax.random.fold_in(key_list[4], 1), 0, 1)
    return dict(act_in=act_in, grad_in=grad_in, weight=weight, gain=gain, preempted=preempted)


EPS = 1e-05

def layer_forward(tokens, weights, gain_row):
    widened = tokens.astype(jnp.float32)
    row_mean = lax.optimization_barrier(jnp.sum(widened, -1)) / D
    variance = lax.optimization_barrier(jnp.sum(widened * widened, -1)) / D - row_mean * row_mean
    inv_std = lax.rsqrt(variance + EPS)
    x_hat = (widened - row_mean[:, None]) * inv_std[:, None]
    normed = (x_hat * gain_row.astype(jnp.float32)).astype(jnp.bfloat16)
    preact = lax.dot_general(normed, weights, (((1,), (1,)), ((), ())), preferred_element_type=jnp.float32)
    layer_out = (widened + jax.nn.gelu(preact)).astype(jnp.bfloat16)
    return (layer_out, preact, normed, x_hat, inv_std)

def reference(act_in, grad_in, weight, gain, preempted):

    def one_section(section_index):
        tokens = lax.dynamic_index_in_dim(act_in, section_index, 0, False)
        weights = lax.dynamic_index_in_dim(weight, section_index, 0, False)
        gain_row = lax.dynamic_index_in_dim(gain, section_index, 0, False)
        layer_out, preact, normed, x_hat, inv_std = layer_forward(tokens, weights, gain_row)
        successor = jnp.minimum(section_index + 1, N_SECTION - 1).astype(jnp.int32)
        next_weights = lax.dynamic_index_in_dim(weight, successor, 0, False)
        next_gain = lax.dynamic_index_in_dim(gain, successor, 0, False)
        redundant = layer_forward(layer_out, next_weights, next_gain)[0]
        flags = lax.dynamic_index_in_dim(preempted, section_index, 0, False)
        active = (flags * (section_index < N_SECTION - 1).astype(jnp.int32)).astype(jnp.float32)
        shadow = (redundant.astype(jnp.float32) * active[:, None]).astype(jnp.bfloat16)
        cotangent = lax.dynamic_index_in_dim(grad_in, section_index, 0, False).astype(jnp.float32)
        _, pullback = jax.vjp(jax.nn.gelu, preact)
        dpre = pullback(cotangent)[0].astype(jnp.bfloat16)
        weight_grad = lax.dot_general(dpre, normed, (((0,), (0,)), ((), ())), preferred_element_type=jnp.float32).astype(jnp.bfloat16)
        dnormed = jnp.dot(dpre, weights, preferred_element_type=jnp.float32)
        gain_grad = lax.optimization_barrier(jnp.sum(dnormed * x_hat, 0))
        dhat = dnormed * gain_row.astype(jnp.float32)
        mean_grad = lax.optimization_barrier(jnp.sum(dhat, -1)) / D
        mean_proj = lax.optimization_barrier(jnp.sum(dhat * x_hat, -1)) / D
        dinput = inv_std[:, None] * (dhat - mean_grad[:, None] - x_hat * mean_proj[:, None])
        input_grad = (cotangent + dinput).astype(jnp.bfloat16)
        return (layer_out, shadow, input_grad, weight_grad, gain_grad)
    outputs, shadow, input_grad, weight_grad, gain_grad = lax.map(one_section, jnp.arange(N_SECTION, dtype=jnp.int32))
    empty_block = jnp.zeros((1, TOKENS, D), jnp.bfloat16)
    next_input = jnp.concatenate([empty_block, outputs[:-1]], 0)
    return (next_input, shadow, input_grad, weight_grad, gain_grad)
```

```python
import functools

import jax
import jax.numpy as jnp
from jax import lax
from jax.experimental import pallas as pl
from jax.experimental.pallas import tpu as pltpu
from jax.sharding import PartitionSpec as P

EPS = 1e-05
MESH = pl.DeviceIdType.MESH
F32 = jnp.float32
BF16 = jnp.bfloat16
LANES = 128
HALF = 64
PAD = 16

NT = (((1,), (1,)), ((), ()))
NN = (((1,), (0,)), ((), ()))


def dot(a, b, dims):
    return lax.dot_general(a, b, dims, preferred_element_type=F32)


def low_lanes(rows):
    return lax.broadcasted_iota(jnp.int32, (rows, LANES), 1) < HALF


def half_turn(value):
    return pltpu.roll(value, HALF, 1)


def split_tiles(value):
    tail = value[:, LANES:]
    return value[:, :LANES], jnp.concatenate([tail, tail], axis=1)


def main_and_rest(value, odd):
    first, tail = split_tiles(value)
    low = low_lanes(value.shape[0])
    turned = half_turn(first)
    main = jnp.where(odd, jnp.where(low, turned, tail), first)
    rest = jnp.where(odd, jnp.where(low, first, turned), tail)
    return main, rest


def pack(value, odd):
    half = value.shape[0] // 2
    main, rest = main_and_rest(value, odd)
    here = low_lanes(half) != odd
    return main, jnp.where(here, rest[:half], rest[half:])


def unpack(main, folded, odd):
    half = folded.shape[0]
    here = low_lanes(half) != odd
    turned = half_turn(folded)
    rest = jnp.concatenate([jnp.where(here, folded, turned), jnp.where(here, turned, folded)], axis=0)
    main_turned = half_turn(main)
    first = jnp.where(odd, jnp.where(low_lanes(main.shape[0]), rest, main_turned), main)
    tail = jnp.where(odd, main_turned, rest)
    return jnp.concatenate([first, tail[:, :HALF]], axis=1)


def gelu_parts(p):
    k = 0.7978845608028654
    t = jnp.tanh(k * (p + 0.044715 * (p * p * p)))
    return t, k * (1.0 + (3.0 * 0.044715) * (p * p))


def eye(rows, columns):
    return lax.broadcasted_iota(jnp.int32, (rows, columns), 0) == lax.broadcasted_iota(
        jnp.int32, (rows, columns), 1
    )


def as_column(row):
    n = row.shape[1]
    return jnp.sum(jnp.where(eye(n, n), jnp.broadcast_to(row, (n, n)), 0.0), axis=1, keepdims=True)


def as_row(column, width):
    n = column.shape[0]
    return jnp.sum(jnp.where(eye(n, width), jnp.broadcast_to(column, (n, width)), 0.0), axis=0, keepdims=True)


COPIES = (
    [(tag, kind, k) for tag in "ab" for kind in "z+-f" for k in range(4) if (kind, k) != ("z", 0)]
    + [(tag, "s", j) for tag in "ab" for j in range(7)]
    + [("next",), ("back",)]
    + [("S", "z", k) for k in (1, 2, 3)]
    + [("S", "x", k) for k in (1, 2, 3)]
    + [("S", "c")]
    + [("C", j) for j in range(4)]
    + [("F", j) for j in range(2)]
    + [("G", j, part) for j in range(2) for part in range(2)]
    + [("Z", k) for k in (1, 2, 3)]
)
COPY_ID = {name: index for index, name in enumerate(COPIES)}


def kernel(
    sections,
    features,
    act,
    grad,
    gain,
    preempted,
    weight,
    next_out,
    shadow_out,
    input_grad_out,
    gain_grad_out,
    weight_grad_out,
    wv,
    wp,
    xs,
    xs2,
    gains,
    got1,
    got2,
    acc,
    squares,
    outgoing,
    returned,
    partial,
    from_sib,
    hop,
    g_in,
    h_out,
    z_in,
    s_own,
    s_z,
    s_x,
    s_xr,
    s_c,
    s_cr,
    mean_s,
    inv_s,
    dpre_s,
    dpre_t,
    stage,
    send_sem,
    recv_sem,
    w_sem,
    out_sem,
):
    T, F = act.shape[1], act.shape[2]
    H = T // 2
    R = T + H
    C = 4 * F
    section, dp, z = lax.axis_index("section"), lax.axis_index("dp"), lax.axis_index("mp")
    core = dp % 2
    sib = dp + 1 - 2 * core
    odd = (z % 2) == 1

    def near(c, step):
        return (c + 2 * step + 8) % 8

    up, down, far = near(dp, 1), near(dp, -1), near(dp, 2)
    to_up, to_down, to_far, to_sib = {"dp": up}, {"dp": down}, {"dp": far}, {"dp": sib}
    to_next = {"section": (section + 1) % sections}
    to_back = {"section": (section + sections - 1) % sections}

    def to_z(k):
        return {"mp": (z + k) % 4}

    def zk(k):
        return (z + 4 - k) % 4

    def rc(name, src, dst, device):
        n = COPY_ID[name]
        return pltpu.make_async_remote_copy(
            src_ref=src,
            dst_ref=dst,
            send_sem=send_sem.at[n],
            recv_sem=recv_sem.at[n],
            device_id=device,
            device_id_type=MESH,
        )

    def send(name, src, dst, device):
        rc(name, src, dst, device).start()

    def arrive(name, dst):
        rc(name, dst, dst, to_sib).wait_recv()

    def sent(name, src):
        rc(name, src, src, to_sib).wait_send()

    def weight_copy(c):
        return pltpu.make_async_copy(
            weight.at[0, :, pl.ds(c * C, C)], wv.at[c], w_sem.at[c]
        )

    for c in range(8):
        weight_copy(c).start()
    barrier = pltpu.get_barrier_semaphore()
    partners = [to_z(1), to_z(2), to_z(3), to_up, to_down, to_far, to_sib, to_next, to_back]
    for device in partners:
        pl.semaphore_signal(barrier, inc=1, device_id=device, device_id_type=MESH)

    x_own = act[0].astype(F32)
    main, folded = pack(x_own, odd)
    got1[dp, z, :T] = main.astype(BF16)
    got1[dp, z, T:R] = folded.astype(BF16)
    gain_row = gain[...].astype(F32)
    g_main, g_rest = main_and_rest(jnp.broadcast_to(gain_row, (PAD, F)), odd)
    first_row = lax.broadcasted_iota(jnp.int32, (PAD, LANES), 0) == 0
    got1[dp, z, R:] = jnp.where(first_row, g_main, g_rest).astype(BF16)
    pl.semaphore_wait(barrier, len(partners))

    def gather_begin(tag, got):
        own = got.at[dp, z]
        for k in (1, 2, 3):
            send((tag, "z", k), own, own, to_z(k))
        send((tag, "+", 0), own, own, to_up)
        send((tag, "-", 0), own, own, to_down)

    gather_begin("a", got1)

    ones = jnp.ones((PAD, C), BF16)

    def fill(c, carry):
        xs[c, T:] = ones
        wp[c, F:] = ones
        return carry

    lax.fori_loop(0, 8, fill, 0)
    xs2[T:] = ones

    def chunk_of(i):
        step = jnp.where(i < 2, 0, jnp.where(i > 5, 2, jnp.where(i % 2 == 0, 3, 1)))
        flip = jnp.where((i == 1) | (i == 4) | (i == 5) | (i == 7), 1, 0)
        mine = (dp + 2 * step) % 8
        return mine + flip * (1 - 2 * core)

    def gather_step(tag, got, i):
        other_up, other_down, other_far = near(sib, 1), near(sib, -1), near(sib, 2)

        @pl.when(i == 0)
        def _():
            for k in (1, 2, 3):
                block = got.at[dp, zk(k)]
                arrive((tag, "z", k), block)
                send((tag, "+", k), block, block, to_up)
                send((tag, "-", k), block, block, to_down)
            send((tag, "s", 0), got.at[dp], got.at[dp], to_sib)

        @pl.when(i == 1)
        def _():
            for k in (0, 1):
                a, b = got.at[down, zk(k)], got.at[up, zk(k)]
                arrive((tag, "+", k), a)
                arrive((tag, "-", k), b)
                if k % 2 == 0:
                    send((tag, "f", k), a, a, to_up)
                else:
                    send((tag, "f", k), b, b, to_down)
            arrive((tag, "s", 0), got.at[sib])

        @pl.when(i == 2)
        def _():
            for k in (2, 3):
                a, b = got.at[down, zk(k)], got.at[up, zk(k)]
                arrive((tag, "+", k), a)
                arrive((tag, "-", k), b)
                if k % 2 == 0:
                    send((tag, "f", k), a, a, to_up)
                else:
                    send((tag, "f", k), b, b, to_down)
            send((tag, "s", 1), got.at[down], got.at[down], to_sib)
            send((tag, "s", 2), got.at[up], got.at[up], to_sib)

        @pl.when(i == 4)
        def _():
            arrive((tag, "s", 1), got.at[other_down])

        @pl.when(i == 5)
        def _():
            arrive((tag, "s", 2), got.at[other_up])

        @pl.when(i == 6)
        def _():
            for k in range(4):
                block = got.at[far, zk(k)]
                arrive((tag, "f", k), block)
                send((tag, "s", 3 + k), block, block, to_sib)

        @pl.when(i == 7)
        def _():
            for k in range(4):
                arrive((tag, "s", 3 + k), got.at[other_far, zk(k)])

    def gather_end(tag, got):
        for k in range(4):
            if k:
                sent((tag, "z", k), got.at[0, 0])
            for kind in "+-f":
                sent((tag, kind, k), got.at[0, 0])
            sent((tag, "s", 3 + k), got.at[0, 0])
        for j in range(3):
            sent((tag, "s", j), got.at[0])

    low = low_lanes(H)

    def unfold_chunk(got, c, keep):
        total = squares[...]
        for p in range(2):
            r0 = got[c, 2 * p, T:R].astype(F32)
            r1 = got[c, 2 * p + 1, T:R].astype(F32)
            middle = jnp.concatenate([jnp.where(low, r0, r1), half_turn(jnp.where(low, r1, r0))], axis=0)
            t0 = got[c, 2 * p, :T]
            t2 = got[c, 2 * p + 1, :T]
            keep(3 * p, t0)
            keep(3 * p + 1, middle.astype(BF16))
            keep(3 * p + 2, t2)
            t0, t2 = t0.astype(F32), t2.astype(F32)
            total = total + (t0 * t0 + middle * middle + t2 * t2)
        squares[...] = total

    acc[...] = jnp.zeros_like(acc)
    squares[...] = jnp.zeros_like(squares)
    for c in range(8):
        weight_copy(c).wait()

    def first_layer(i, carry):
        gather_step("a", got1, i)
        c = chunk_of(i)
        row_low = low_lanes(1)
        for p in range(2):
            g0 = got1[c, 2 * p, R:].astype(F32)
            g1 = got1[c, 2 * p + 1, R:].astype(F32)
            for j, row in enumerate((g0[0:1], jnp.where(row_low, g0[1:2], g1[1:2]), g1[0:1])):
                gains[c, :, (3 * p + j) * LANES : (3 * p + j + 1) * LANES] = jnp.broadcast_to(row, (8, LANES))
        wp[c, :F] = (wv[c].astype(F32) * gains[c, 0:1]).astype(BF16)

        def keep(t, value):
            xs[c, :T, t * LANES : (t + 1) * LANES] = value

        unfold_chunk(got1, c, keep)
        acc[...] += dot(xs[c], wp[c], NT)
        return carry

    lax.fori_loop(0, 8, first_layer, 0)

    def row_statistics():
        mean = acc[:T, F : F + 1] / features
        variance = jnp.sum(squares[...], axis=1, keepdims=True) / features - mean * mean
        return mean, lax.rsqrt(variance + EPS)

    mean, inv_std = row_statistics()
    weight_sums = acc[T : T + 1, :F]
    preact = inv_std * (acc[:T, :F] - mean * weight_sums)
    t, slope = gelu_parts(preact)
    layer_out = x_own + 0.5 * preact * (1.0 + t)
    main, folded = pack(layer_out.astype(BF16).astype(F32), odd)
    outgoing[:T] = main.astype(BF16)
    outgoing[T:] = folded.astype(BF16)
    send(("next",), outgoing, got2.at[dp, z], to_next)

    derivative = 0.5 * (1.0 + t) + 0.5 * preact * (1.0 - t * t) * slope
    dpre = (grad[0].astype(F32) * derivative).astype(BF16)
    dpre_s[...] = dpre
    dpre_f = dpre.astype(F32)
    mean_s[...] = jnp.broadcast_to(mean, (T, LANES))
    inv_s[...] = jnp.broadcast_to(inv_std, (T, LANES))
    sum_grad = jnp.sum(dpre_f * weight_sums, axis=1, keepdims=True)
    sum_proj = jnp.sum(dpre_f * preact, axis=1, keepdims=True)
    width = s_own.shape[1]
    row_is_0 = lax.broadcasted_iota(jnp.int32, (8, width), 0) == 0
    s_own[...] = jnp.where(row_is_0, as_row(sum_grad, width), as_row(sum_proj, width))
    for k in (1, 2, 3):
        send(("S", "z", k), s_own, s_z.at[k - 1], to_z(k))
    dpre_t[...] = dot(jnp.where(eye(F, F), 1.0, 0.0).astype(BF16), dpre, NT).astype(BF16)

    def partial_chunk(c):
        product = dot(dpre_s[...], wv[c], NN)
        for p in range(2):
            tile = [product[:, (3 * p + j) * LANES : (3 * p + j + 1) * LANES] for j in range(3)]
            top, bottom = tile[1][:H], half_turn(tile[1][H:])
            partial[c, 2 * p, :T] = tile[0].astype(BF16)
            partial[c, 2 * p, T:] = jnp.where(low, top, bottom).astype(BF16)
            partial[c, 2 * p + 1, :T] = tile[2].astype(BF16)
            partial[c, 2 * p + 1, T:] = jnp.where(low, bottom, top).astype(BF16)

    def x_of(j):
        return (dp // 2 + jnp.where(j == 0, 2, jnp.where(j == 1, 1, jnp.where(j == 2, 3, 0)))) % 4

    def partial_step(i, carry):
        j = i % 4
        theirs = i < 4
        x = x_of(j)
        c = 2 * x + jnp.where(theirs, 1 - core, core)
        partial_chunk(c)
        for n in range(4):

            @pl.when(i == n)
            def _():
                send(("C", n), partial.at[c], from_sib.at[x], to_sib)

        return carry

    lax.fori_loop(0, 8, partial_step, 0)

    def fold_in(c, source, index, first=0, count=4):
        for b in range(first, first + count):
            partial[c, b] = (partial[c, b].astype(F32) + source[index, b - first].astype(F32)).astype(BF16)

    def weight_grad_copy(c):
        return pltpu.make_async_copy(
            stage.at[c], weight_grad_out.at[0, :, pl.ds(pl.multiple_of(c * C, C), C)], out_sem.at[c]
        )

    def weight_grad_chunk(c):
        x = xs[c, :T].astype(F32)
        normed = ((x - mean_s[:, 0:1]) * inv_s[:, 0:1] * gains[c, 0:1]).astype(BF16)
        stage[c] = dot(dpre_t[...], normed, NN).astype(BF16)
        weight_grad_copy(c).start()

    arrive(("next",), got2.at[dp, z])
    gather_begin("b", got2)

    def from_sibling(n):
        x = x_of(n)
        arrive(("C", n), from_sib.at[x])
        fold_in(2 * x + core, from_sib, x)

    def second_layer(i, carry):
        gather_step("b", got2, i)

        @pl.when(i == 1)
        def _():
            from_sibling(0)
            send(("F", 0), partial.at[far, 0:2], hop.at[0], to_up)
            send(("F", 1), partial.at[far, 2:4], hop.at[1], to_down)
            for n in (1, 2, 3):
                from_sibling(n)
            send(("G", 0, 0), partial.at[up, 2:4], g_in.at[0, 2:4], to_up)
            send(("G", 1, 0), partial.at[down, 0:2], g_in.at[1, 0:2], to_down)

        @pl.when(i == 2)
        def _():
            for k in (1, 2, 3):
                arrive(("S", "z", k), s_z.at[k - 1])
            s_x[...] = s_own[...] + (s_z[0] + s_z[1] + s_z[2])
            for k in (1, 2, 3):
                send(("S", "x", k), s_x, s_xr.at[k - 1], {"dp": near(dp, k)})

        @pl.when(i == 4)
        def _():
            arrive(("F", 0), hop.at[0])
            fold_in(up, hop, 0, 0, 2)
            send(("G", 0, 1), partial.at[up, 0:2], g_in.at[0, 0:2], to_up)
            arrive(("F", 1), hop.at[1])
            fold_in(down, hop, 1, 2, 2)
            send(("G", 1, 1), partial.at[down, 2:4], g_in.at[1, 2:4], to_down)

        @pl.when(i == 5)
        def _():
            for k in (1, 2, 3):
                arrive(("S", "x", k), s_xr.at[k - 1])
            s_c[...] = s_x[...] + (s_xr[0] + s_xr[1] + s_xr[2])
            send(("S", "c"), s_c, s_cr, to_sib)

        weight_grad_chunk(i)
        c = chunk_of(i)

        def keep(t, value):
            xs2[:T, t * LANES : (t + 1) * LANES] = value

        unfold_chunk(got2, c, keep)
        acc[...] += dot(xs2[...], wp[c], NT)
        return carry

    acc[...] = jnp.zeros_like(acc)
    squares[...] = jnp.zeros_like(squares)
    lax.fori_loop(0, 8, second_layer, 0)

    mean2, inv_std2 = row_statistics()
    preact2 = inv_std2 * (acc[:T, :F] - mean2 * acc[T : T + 1, :F])
    t2, _ = gelu_parts(preact2)
    x_next = unpack(got2[dp, z, :T].astype(F32), got2[dp, z, T:].astype(F32), odd)
    redundant = (x_next + 0.5 * preact2 * (1.0 + t2)).astype(BF16).astype(F32)
    main, folded = pack(redundant, odd)
    sent(("next",), outgoing)
    outgoing[:T] = main.astype(BF16)
    outgoing[T:] = folded.astype(BF16)
    send(("back",), outgoing, returned, to_back)
    next_out[0] = jnp.where(section > 0, x_next, 0.0).astype(BF16)

    for j in range(2):
        for part in range(2):
            half = g_in.at[j, 0:2] if j == part ^ 1 else g_in.at[j, 2:4]
            arrive(("G", j, part), half)

    def sum_x(b):
        return partial[dp, b].astype(F32) + (g_in[0, b].astype(F32) + g_in[1, b].astype(F32))

    for k in (1, 2, 3):
        b = (z + k) % 4
        h_out[k - 1] = sum_x(b).astype(BF16)
        send(("Z", k), h_out.at[k - 1], z_in.at[k - 1], to_z(k))
    total = sum_x(z)
    for k in (1, 2, 3):
        arrive(("Z", k), z_in.at[k - 1])
        total = total + z_in[k - 1].astype(F32)
    dnormed = unpack(total[:T], total[T:], odd)

    arrive(("S", "c"), s_cr)
    sums = (s_c[...] + s_cr[...])[:, :T] / features
    mean_grad = as_column(sums[0:1])
    mean_proj = as_column(sums[1:2])
    inv_std = inv_s[:, 0:1]
    x_hat = (act[0].astype(F32) - mean_s[:, 0:1]) * inv_std
    gain_grad_out[...] = jnp.sum(dnormed * x_hat, axis=0, keepdims=True)
    dhat = dnormed * gain[...].astype(F32)
    dinput = inv_std * (dhat - mean_grad - x_hat * mean_proj)
    input_grad_out[0] = (grad[0].astype(F32) + dinput).astype(BF16)

    active = as_column(preempted[...].astype(F32)) * jnp.where(section < sections - 1, 1.0, 0.0)
    arrive(("back",), returned)
    shadow = unpack(returned[:T].astype(F32), returned[T:].astype(F32), odd)
    shadow_out[0] = (shadow * active).astype(BF16)

    gather_end("a", got1)
    gather_end("b", got2)
    sent(("back",), outgoing)
    for k in (1, 2, 3):
        sent(("S", "z", k), s_own)
        sent(("S", "x", k), s_x)
        sent(("Z", k), h_out.at[k - 1])
    sent(("S", "c"), s_c)
    for n in range(4):
        sent(("C", n), partial.at[0])
    for j in range(2):
        sent(("F", j), hop.at[0])
        for part in range(2):
            sent(("G", j, part), hop.at[0])
    for c in range(8):
        weight_grad_copy(c).wait()


def shards(sections, devices, act_in, grad_in, weight, gain, preempted):
    _, T, F = act_in.shape
    D = weight.shape[2]
    R = T + T // 2
    C = 4 * F
    vmem, anywhere = pl.BlockSpec(memory_space=pltpu.VMEM), pl.BlockSpec(memory_space=pl.ANY)
    shape = jax.ShapeDtypeStruct
    copies = len(COPIES)
    results = pl.pallas_call(
        functools.partial(kernel, sections, float(D)),
        out_shape=(
            shape((1, T, F), BF16),
            shape((1, T, F), BF16),
            shape((1, T, F), BF16),
            shape((1, F), F32),
            shape((1, F, D), BF16),
        ),
        in_specs=[vmem, vmem, vmem, vmem, anywhere],
        out_specs=(vmem, vmem, vmem, vmem, anywhere),
        scratch_shapes=[
            pltpu.VMEM((8, F, C), BF16),
            pltpu.VMEM((8, F + PAD, C), BF16),
            pltpu.VMEM((8, T + PAD, C), BF16),
            pltpu.VMEM((T + PAD, C), BF16),
            pltpu.VMEM((8, 8, C), F32),
            pltpu.VMEM((8, 4, R + PAD, LANES), BF16),
            pltpu.VMEM((8, 4, R, LANES), BF16),
            pltpu.VMEM((T + PAD, F + PAD), F32),
            pltpu.VMEM((T, LANES), F32),
            pltpu.VMEM((R, LANES), BF16),
            pltpu.VMEM((R, LANES), BF16),
            pltpu.VMEM((8, 4, R, LANES), BF16),
            pltpu.VMEM((4, 4, R, LANES), BF16),
            pltpu.VMEM((2, 2, R, LANES), BF16),
            pltpu.VMEM((2, 4, R, LANES), BF16),
            pltpu.VMEM((3, R, LANES), BF16),
            pltpu.VMEM((3, R, LANES), BF16),
            pltpu.VMEM((8, 256), F32),
            pltpu.VMEM((3, 8, 256), F32),
            pltpu.VMEM((8, 256), F32),
            pltpu.VMEM((3, 8, 256), F32),
            pltpu.VMEM((8, 256), F32),
            pltpu.VMEM((8, 256), F32),
            pltpu.VMEM((T, LANES), F32),
            pltpu.VMEM((T, LANES), F32),
            pltpu.VMEM((T, F), BF16),
            pltpu.VMEM((F, T), BF16),
            pltpu.VMEM((8, F, C), BF16),
            pltpu.SemaphoreType.DMA((copies,)),
            pltpu.SemaphoreType.DMA((copies,)),
            pltpu.SemaphoreType.DMA((8,)),
            pltpu.SemaphoreType.DMA((8,)),
        ],
        compiler_params=pltpu.CompilerParams(
            collective_id=0, has_side_effects=True, vmem_limit_bytes=40 * 1024 * 1024
        ),
    )(act_in, grad_in, gain, preempted, weight)
    next_input, shadow, input_grad, gain_grad, weight_grad = results
    return next_input, shadow, input_grad, weight_grad, gain_grad


def solution(mesh):
    return jax.shard_map(
        functools.partial(shards, mesh.shape["section"], mesh.shape["dp"] * mesh.shape["mp"]),
        mesh=mesh,
        in_specs=(
            P("section", None, ("dp", "mp")),
            P("section", None, ("dp", "mp")),
            P("section", ("dp", "mp"), None),
            P("section", ("dp", "mp")),
            P("section", None),
        ),
        out_specs=(
            P("section", None, ("dp", "mp")),
            P("section", None, ("dp", "mp")),
            P("section", None, ("dp", "mp")),
            P("section", ("dp", "mp"), None),
            P("section", ("dp", "mp")),
        ),
        check_vma=False,
    )
```

```python
import functools

import jax
import jax.numpy as jnp
from jax import lax
from jax.experimental import pallas as pl
from jax.experimental.pallas import tpu as pltpu
from jax.sharding import PartitionSpec as P

EPS = 1e-05
MESH = pl.DeviceIdType.MESH
F32 = jnp.float32
BF16 = jnp.bfloat16
LANES = 128
HALF = 64
PAD = 16

NT = (((1,), (1,)), ((), ()))
NN = (((1,), (0,)), ((), ()))


def dot(a, b, dims):
    return lax.dot_general(a, b, dims, preferred_element_type=F32)


def low_lanes(rows):
    return lax.broadcasted_iota(jnp.int32, (rows, LANES), 1) < HALF


def half_turn(value):
    return pltpu.roll(value, HALF, 1)


def split_tiles(value):
    tail = value[:, LANES:]
    return value[:, :LANES], jnp.concatenate([tail, tail], axis=1)


def main_and_rest(value, odd):
    first, tail = split_tiles(value)
    low = low_lanes(value.shape[0])
    turned = half_turn(first)
    main = jnp.where(odd, jnp.where(low, turned, tail), first)
    rest = jnp.where(odd, jnp.where(low, first, turned), tail)
    return main, rest


def pack(value, odd):
    half = value.shape[0] // 2
    main, rest = main_and_rest(value, odd)
    here = low_lanes(half) != odd
    return main, jnp.where(here, rest[:half], rest[half:])


def unpack(main, folded, odd):
    half = folded.shape[0]
    here = low_lanes(half) != odd
    turned = half_turn(folded)
    rest = jnp.concatenate([jnp.where(here, folded, turned), jnp.where(here, turned, folded)], axis=0)
    main_turned = half_turn(main)
    first = jnp.where(odd, jnp.where(low_lanes(main.shape[0]), rest, main_turned), main)
    tail = jnp.where(odd, main_turned, rest)
    return jnp.concatenate([first, tail[:, :HALF]], axis=1)


def gelu_parts(p):
    k = 0.7978845608028654
    t = jnp.tanh(k * (p + 0.044715 * (p * p * p)))
    return t, k * (1.0 + (3.0 * 0.044715) * (p * p))


def eye(rows, columns):
    return lax.broadcasted_iota(jnp.int32, (rows, columns), 0) == lax.broadcasted_iota(
        jnp.int32, (rows, columns), 1
    )


def as_column(row):
    n = row.shape[1]
    return jnp.sum(jnp.where(eye(n, n), jnp.broadcast_to(row, (n, n)), 0.0), axis=1, keepdims=True)


def as_row(column, width, start):
    n = column.shape[0]
    here = lax.broadcasted_iota(jnp.int32, (n, width), 0) + start == lax.broadcasted_iota(jnp.int32, (n, width), 1)
    return jnp.sum(jnp.where(here, jnp.broadcast_to(column, (n, width)), 0.0), axis=0, keepdims=True)


GROUPS = 2
SPLIT = (96, 64)
COPIES = (
    [(tag, g, "z", k) for tag in "ab" for g in range(GROUPS) for k in (1, 2, 3)]
    + [(tag, g, kind, k) for tag in "ab" for g in range(GROUPS) for kind in "+-s" for k in range(4)]
    + [(tag, g, "f", k) for tag in "ab" for g in range(GROUPS) for k in range(4)]
    + [(name, g) for name in ("next", "back") for g in range(GROUPS)]
    + [("S", "z", k) for k in (1, 2, 3)]
    + [("S", "x", k) for k in (1, 2, 3)]
    + [("S", "c")]
    + [("C", g, j) for g in range(GROUPS) for j in range(4)]
    + [("F", g, j) for g in range(GROUPS) for j in range(2)]
    + [("G", g, j, part) for g in range(GROUPS) for j in range(2) for part in range(2)]
    + [("Z", g, k) for g in range(GROUPS) for k in (1, 2, 3)]
)
COPY_ID = {name: index for index, name in enumerate(COPIES)}


def kernel(
    sections,
    features,
    act,
    grad,
    gain,
    preempted,
    weight,
    next_out,
    shadow_out,
    input_grad_out,
    gain_grad_out,
    weight_grad_out,
    act_v,
    grad_v,
    gain_v,
    preempted_v,
    wv,
    wp,
    xs,
    xs2,
    gains,
    got1,
    got2,
    acc,
    squares,
    outgoing,
    returned,
    partial,
    from_sib,
    hop,
    g_in,
    h_out,
    z_in,
    s_own,
    s_z,
    s_x,
    s_xr,
    s_c,
    s_cr,
    sums_s,
    mean_s,
    inv_s,
    dpre_s,
    dpre_t,
    send_sem,
    recv_sem,
    w_sem,
    in_sem,
):
    T, F = act.shape[1], act.shape[2]
    C = 4 * F
    count = [SPLIT[0], T - SPLIT[0]]
    start = [0, SPLIT[0]]
    rows = [slice(start[g], start[g] + count[g]) for g in range(GROUPS)]
    folded = [n + n // 2 for n in count]
    section, dp, z = lax.axis_index("section"), lax.axis_index("dp"), lax.axis_index("mp")
    core = dp % 2
    sib = dp + 1 - 2 * core
    odd = (z % 2) == 1

    def near(c, step):
        return (c + 2 * step + 8) % 8

    up, down, far = near(dp, 1), near(dp, -1), near(dp, 2)
    to_up, to_down, to_far, to_sib = {"dp": up}, {"dp": down}, {"dp": far}, {"dp": sib}
    to_next = {"section": (section + 1) % sections}
    to_back = {"section": (section + sections - 1) % sections}

    def to_z(k):
        return {"mp": (z + k) % 4}

    def zk(k):
        return (z + 4 - k) % 4

    def rc(name, src, dst, device):
        n = COPY_ID[name]
        return pltpu.make_async_remote_copy(
            src_ref=src,
            dst_ref=dst,
            send_sem=send_sem.at[n],
            recv_sem=recv_sem.at[n],
            device_id=device,
            device_id_type=MESH,
        )

    def send(name, src, dst, device):
        rc(name, src, dst, device).start()

    def arrive(name, dst):
        rc(name, dst, dst, to_sib).wait_recv()

    def sent(name, src):
        rc(name, src, src, to_sib).wait_send()

    small = [
        pltpu.make_async_copy(src, dst, in_sem.at[n])
        for n, (src, dst) in enumerate(
            ((act, act_v), (gain, gain_v), (grad, grad_v), (preempted, preempted_v))
        )
    ]

    def weight_copy(c):
        return pltpu.make_async_copy(weight.at[0, :, pl.ds(c * C, C)], wv.at[c], w_sem.at[c])

    for copy in small:
        copy.start()
    barrier = pltpu.get_barrier_semaphore()
    partners = [to_z(1), to_z(2), to_z(3), to_up, to_down, to_far, to_sib, to_next, to_back]
    for device in partners:
        pl.semaphore_signal(barrier, inc=1, device_id=device, device_id_type=MESH)
    for c in range(8):
        weight_copy(c).start()

    small[0].wait()
    small[1].wait()
    x_own = act_v[0].astype(F32)

    def put(block, g, value):
        main, fold = pack(value, odd)
        block[: count[g]] = main.astype(BF16)
        block[count[g] : folded[g]] = fold.astype(BF16)

    for g in range(GROUPS):
        put(got1[g].at[dp, z], g, x_own[rows[g]])
    gain_row = gain_v[...].astype(F32)
    g_main, g_rest = main_and_rest(jnp.broadcast_to(gain_row, (PAD, F)), odd)
    first_row = lax.broadcasted_iota(jnp.int32, (PAD, LANES), 0) == 0
    got1[0][dp, z, folded[0] :] = jnp.where(first_row, g_main, g_rest).astype(BF16)
    pl.semaphore_wait(barrier, len(partners))

    def own_to_z(tag, g, got):
        own = got.at[dp, z]
        for k in (1, 2, 3):
            send((tag, g, "z", k), own, own, to_z(k))

    def own_to_x(tag, g, got):
        own = got.at[dp, z]
        send((tag, g, "+", 0), own, own, to_up)
        send((tag, g, "-", 0), own, own, to_down)
        if tag == "a":
            send((tag, g, "f", 0), own, own, to_far)

    def from_z(tag, g, got, k):
        block = got.at[dp, zk(k)]
        arrive((tag, g, "z", k), block)
        send((tag, g, "+", k), block, block, to_up)
        send((tag, g, "-", k), block, block, to_down)
        if k == 3:
            send((tag, g, "f", 3), block, block, to_far)
            send((tag, g, "s", 0), got.at[dp], got.at[dp], to_sib)

    def from_x(tag, g, got, k):
        a, b = got.at[down, zk(k)], got.at[up, zk(k)]
        arrive((tag, g, "+", k), a)
        arrive((tag, g, "-", k), b)
        if k == 3:
            send((tag, g, "s", 1), got.at[down], got.at[down], to_sib)
            send((tag, g, "s", 2), got.at[up], got.at[up], to_sib)
        elif tag == "a" and k == 0:
            pass
        elif (k + g) % 2 == 0:
            send((tag, g, "f", k), a, a, to_up)
        else:
            send((tag, g, "f", k), b, b, to_down)

    def from_far(tag, g, got):
        for k in range(4):
            arrive((tag, g, "f", k), got.at[far, zk(k)])
        send((tag, g, "s", 3), got.at[far], got.at[far], to_sib)

    def from_sib_core(tag, g, got, j):
        arrive((tag, g, "s", j), got.at[near(sib, (0, -1, 1, 2)[j])])

    def gather_end(tag, g, got):
        for k in range(4):
            if k:
                sent((tag, g, "z", k), got.at[0, 0])
            for kind in "+-f":
                sent((tag, g, kind, k), got.at[0, 0])
            sent((tag, g, "s", k), got.at[0])

    def chunk_of(i):
        step = jnp.where(i < 2, 0, jnp.where(i > 5, 2, jnp.where(i % 2 == 0, 3, 1)))
        flip = jnp.where((i == 1) | (i == 4) | (i == 5) | (i == 7), 1, 0)
        mine = (dp + 2 * step) % 8
        return mine + flip * (1 - 2 * core)

    def steps(work, events):
        def body(i, carry):
            for n in sorted(events):

                @pl.when(i == n)
                def _():
                    for action, *arguments in events[n]:
                        action(*arguments)

            work(i)
            return carry

        lax.fori_loop(0, 8, body, 0)

    def gather_events(tag, got, extra):
        def z(g, k):
            return (from_z, tag, g, got[g], k)

        def x(g, k):
            return (from_x, tag, g, got[g], k)

        def s(g, j):
            return (from_sib_core, tag, g, got[g], j)

        def f(g):
            return (from_far, tag, g, got[g])

        first = {
            0: [z(0, 1), (own_to_z, tag, 1, got[1]), x(0, 0), z(0, 2), z(0, 3)],
            1: [x(0, 1), z(1, 1), s(0, 0)],
            2: [x(0, 2), z(1, 2), x(1, 0), x(0, 3), z(1, 3)],
            4: [x(1, 1), s(0, 1)],
            5: [x(1, 2), s(0, 2)],
            6: [f(0)],
            7: [x(1, 3), s(0, 3)],
        }
        second = {
            1: [s(1, 0)],
            4: [s(1, 1)],
            5: [s(1, 2)],
            6: [f(1)],
            7: [s(1, 3)],
        }
        for (g, n), actions in extra.items():
            events = (first, second)[g]
            events[n] = events.get(n, []) + actions
        return first, second

    own_to_z("a", 0, got1[0])
    for g in range(GROUPS):
        own_to_x("a", g, got1[g])

    ones = jnp.ones((PAD, C), BF16)

    def fill(c, carry):
        xs[c, :PAD] = ones
        wp[c, F:] = ones
        return carry

    lax.fori_loop(0, 8, fill, 0)

    low = [low_lanes(n // 2) for n in count]

    def unfold_chunk(got, g, c, keep):
        n, m = count[g], folded[g]
        total = squares[rows[g]]
        for p in range(2):
            r0 = got[c, 2 * p, n:m].astype(F32)
            r1 = got[c, 2 * p + 1, n:m].astype(F32)
            middle = jnp.concatenate(
                [jnp.where(low[g], r0, r1), half_turn(jnp.where(low[g], r1, r0))], axis=0
            )
            t0 = got[c, 2 * p, :n]
            t2 = got[c, 2 * p + 1, :n]
            keep(3 * p, t0)
            keep(3 * p + 1, middle.astype(BF16))
            keep(3 * p + 2, t2)
            t0, t2 = t0.astype(F32), t2.astype(F32)
            total = total + (t0 * t0 + middle * middle + t2 * t2)
        squares[rows[g]] = total

    spot = [slice(PAD + start[g], PAD + start[g] + count[g]) for g in range(GROUPS)]
    fed = [slice(0, PAD + count[0]), spot[1]]

    def first_layer(g):
        def work(i):
            c = chunk_of(i)
            if g == 0:
                row_low = low_lanes(1)
                for p in range(2):
                    g0 = got1[0][c, 2 * p, folded[0] :].astype(F32)
                    g1 = got1[0][c, 2 * p + 1, folded[0] :].astype(F32)
                    for j, row in enumerate((g0[0:1], jnp.where(row_low, g0[1:2], g1[1:2]), g1[0:1])):
                        gains[c, :, (3 * p + j) * LANES : (3 * p + j + 1) * LANES] = jnp.broadcast_to(
                            row, (8, LANES)
                        )
                wp[c, :F] = (wv[c].astype(F32) * gains[c, 0:1]).astype(BF16)

            def keep(t, value):
                xs[c, spot[g], t * LANES : (t + 1) * LANES] = value

            unfold_chunk(got1[g], g, c, keep)
            acc[fed[g]] += dot(xs[c, fed[g]], wp[c], NT)

        return work

    def second_layer(g):
        def work(i):
            c = chunk_of(i)

            def keep(t, value):
                xs2[: count[g], t * LANES : (t + 1) * LANES] = value

            unfold_chunk(got2[g], g, c, keep)
            acc[spot[g]] += dot(xs2[: count[g]], wp[c], NT)

        return work

    def row_statistics(g):
        mean = acc[spot[g], F : F + 1] / features
        variance = jnp.sum(squares[rows[g]], axis=1, keepdims=True) / features - mean * mean
        return mean, lax.rsqrt(variance + EPS)

    width = s_own.shape[1]
    row_is_0 = lax.broadcasted_iota(jnp.int32, (8, width), 0) == 0

    def finish_first(g):
        mean, inv_std = row_statistics(g)
        if g == 0:
            sums_s[...] = acc[0:8, :F]
        weight_sums = sums_s[0:1]
        preact = inv_std * (acc[spot[g], :F] - mean * weight_sums)
        t, slope = gelu_parts(preact)
        x = act_v[0, rows[g]].astype(F32)
        layer_out = x + 0.5 * preact * (1.0 + t)
        put(outgoing[g], g, layer_out.astype(BF16).astype(F32))
        send(("next", g), outgoing[g], got2[g].at[dp, z], to_next)

        derivative = 0.5 * (1.0 + t) + 0.5 * preact * (1.0 - t * t) * slope
        dpre = (grad_v[0, rows[g]].astype(F32) * derivative).astype(BF16)
        dpre_s[rows[g]] = dpre
        dpre_f = dpre.astype(F32)
        mean_s[rows[g]] = jnp.broadcast_to(mean, (count[g], LANES))
        inv_s[rows[g]] = jnp.broadcast_to(inv_std, (count[g], LANES))
        sum_grad = as_row(jnp.sum(dpre_f * weight_sums, axis=1, keepdims=True), width, start[g])
        sum_proj = as_row(jnp.sum(dpre_f * preact, axis=1, keepdims=True), width, start[g])
        both = jnp.where(row_is_0, sum_grad, sum_proj)
        s_own[...] = both if g == 0 else s_own[...] + both

    def finish_second(g):
        mean, inv_std = row_statistics(g)
        preact = inv_std * (acc[spot[g], :F] - mean * sums_s[0:1])
        t, _ = gelu_parts(preact)
        own = got2[g].at[dp, z]
        x = unpack(own[: count[g]].astype(F32), own[count[g] :].astype(F32), odd)
        redundant = (x + 0.5 * preact * (1.0 + t)).astype(BF16).astype(F32)
        sent(("next", g), outgoing[g])
        put(outgoing[g], g, redundant)
        send(("back", g), outgoing[g], returned[g], to_back)
        next_out[0, rows[g]] = jnp.where(section > 0, x, 0.0).astype(BF16)

    def x_of(j):
        return (dp // 2 + jnp.where(j == 0, 2, jnp.where(j == 1, 1, jnp.where(j == 2, 3, 0)))) % 4

    def partial_sums(g):
        n, h = count[g], count[g] // 2

        def body(i, carry):
            j = i % 4
            theirs = i < 4
            x = x_of(j)
            c = 2 * x + jnp.where(theirs, 1 - core, core)
            product = dot(dpre_s[rows[g]], wv[c], NN)
            for p in range(2):
                tile = [product[:, (3 * p + q) * LANES : (3 * p + q + 1) * LANES] for q in range(3)]
                top, bottom = tile[1][:h], half_turn(tile[1][h:])
                partial[g][c, 2 * p, :n] = tile[0].astype(BF16)
                partial[g][c, 2 * p, n:] = jnp.where(low[g], top, bottom).astype(BF16)
                partial[g][c, 2 * p + 1, :n] = tile[2].astype(BF16)
                partial[g][c, 2 * p + 1, n:] = jnp.where(low[g], bottom, top).astype(BF16)
            for m in range(4):

                @pl.when(i == m)
                def _():
                    send(("C", g, m), partial[g].at[c], from_sib[g].at[x], to_sib)

            return carry

        lax.fori_loop(0, 8, body, 0)

    def fold_in(g, c, source, index, first, blocks):
        for b in range(blocks):
            partial[g][c, first + b] = (
                partial[g][c, first + b].astype(F32) + source[index, b].astype(F32)
            ).astype(BF16)

    def from_sibling(g, n):
        x = x_of(n)
        arrive(("C", g, n), from_sib[g].at[x])
        fold_in(g, 2 * x + core, from_sib[g], x, 0, 4)

    def reduce_begin(g):
        from_sibling(g, 0)
        send(("F", g, 0), partial[g].at[far, 0:2], hop[g].at[0], to_up)
        send(("F", g, 1), partial[g].at[far, 2:4], hop[g].at[1], to_down)
        from_sibling(g, 1)
        send(("G", g, 0, 0), partial[g].at[up, 2:4], g_in[g].at[0, 2:4], to_up)
        from_sibling(g, 2)
        send(("G", g, 1, 0), partial[g].at[down, 0:2], g_in[g].at[1, 0:2], to_down)
        from_sibling(g, 3)

    def reduce_hop(g):
        arrive(("F", g, 0), hop[g].at[0])
        fold_in(g, up, hop[g], 0, 0, 2)
        send(("G", g, 0, 1), partial[g].at[up, 0:2], g_in[g].at[0, 0:2], to_up)
        arrive(("F", g, 1), hop[g].at[1])
        fold_in(g, down, hop[g], 1, 2, 2)
        send(("G", g, 1, 1), partial[g].at[down, 2:4], g_in[g].at[1, 2:4], to_down)

    def sum_x(g, b):
        return partial[g][dp, b].astype(F32) + (g_in[g][0, b].astype(F32) + g_in[g][1, b].astype(F32))

    def reduce_z(g):
        arrive(("G", g, 0, 0), g_in[g].at[0, 2:4])
        arrive(("G", g, 1, 0), g_in[g].at[1, 0:2])
        arrive(("G", g, 0, 1), g_in[g].at[0, 0:2])
        arrive(("G", g, 1, 1), g_in[g].at[1, 2:4])
        for k in (1, 2, 3):
            h_out[g][k - 1] = sum_x(g, (z + k) % 4).astype(BF16)
            send(("Z", g, k), h_out[g].at[k - 1], z_in[g].at[k - 1], to_z(k))

    def reduce_end(g):
        total = sum_x(g, z)
        for k in (1, 2, 3):
            arrive(("Z", g, k), z_in[g].at[k - 1])
            total = total + z_in[g][k - 1].astype(F32)
        return unpack(total[: count[g]], total[count[g] :], odd)

    def sums_x():
        for k in (1, 2, 3):
            arrive(("S", "z", k), s_z.at[k - 1])
        s_x[...] = s_own[...] + (s_z[0] + s_z[1] + s_z[2])
        for k in (1, 2, 3):
            send(("S", "x", k), s_x, s_xr.at[k - 1], {"dp": near(dp, k)})

    def sums_core():
        for k in (1, 2, 3):
            arrive(("S", "x", k), s_xr.at[k - 1])
        s_c[...] = s_x[...] + (s_xr[0] + s_xr[1] + s_xr[2])
        send(("S", "c"), s_c, s_cr, to_sib)

    def weight_grad_chunk(c, carry):
        x = xs[c, PAD:].astype(F32)
        normed = ((x - mean_s[:, 0:1]) * inv_s[:, 0:1] * gains[c, 0:1]).astype(BF16)
        weight_grad_out[0, :, pl.ds(pl.multiple_of(c * C, C), C)] = dot(dpre_t[...], normed, NN).astype(BF16)
        return carry

    acc[...] = jnp.zeros_like(acc)
    squares[...] = jnp.zeros_like(squares)
    for c in range(8):
        weight_copy(c).wait()
    small[2].wait()
    small[3].wait()
    events = gather_events("a", got1, {(1, 1): [(reduce_begin, 0)]})
    steps(first_layer(0), events[0])
    finish_first(0)
    partial_sums(0)
    steps(first_layer(1), events[1])
    finish_first(1)
    for k in (1, 2, 3):
        send(("S", "z", k), s_own, s_z.at[k - 1], to_z(k))
    partial_sums(1)
    acc[...] = jnp.zeros_like(acc)
    squares[...] = jnp.zeros_like(squares)
    reduce_begin(1)

    arrive(("next", 0), got2[0].at[dp, z])
    own_to_z("b", 0, got2[0])
    own_to_x("b", 0, got2[0])
    dpre_t[...] = dot(jnp.where(eye(F, F), 1.0, 0.0).astype(BF16), dpre_s[...], NT).astype(BF16)
    lax.fori_loop(0, 6, weight_grad_chunk, 0)
    reduce_hop(0)
    arrive(("next", 1), got2[1].at[dp, z])
    own_to_x("b", 1, got2[1])
    sums_x()
    events = gather_events(
        "b",
        got2,
        {(0, 6): [(sums_core,)], (0, 7): [(reduce_hop, 1)]},
    )
    steps(second_layer(0), events[0])
    finish_second(0)
    lax.fori_loop(6, 8, weight_grad_chunk, 0)
    steps(second_layer(1), events[1])
    finish_second(1)
    for g in range(GROUPS):
        reduce_z(g)

    dnormed = jnp.concatenate([reduce_end(g) for g in range(GROUPS)], axis=0)
    arrive(("S", "c"), s_cr)
    sums = (s_c[...] + s_cr[...])[:, :T] / features
    mean_grad = as_column(sums[0:1])
    mean_proj = as_column(sums[1:2])
    inv_std = inv_s[:, 0:1]
    x_hat = (act_v[0].astype(F32) - mean_s[:, 0:1]) * inv_std
    gain_grad_out[...] = jnp.sum(dnormed * x_hat, axis=0, keepdims=True)
    dhat = dnormed * gain_v[...].astype(F32)
    dinput = inv_std * (dhat - mean_grad - x_hat * mean_proj)
    input_grad_out[0] = (grad_v[0].astype(F32) + dinput).astype(BF16)

    active = as_column(preempted_v[...].astype(F32)) * jnp.where(section < sections - 1, 1.0, 0.0)
    for g in range(GROUPS):
        arrive(("back", g), returned[g])
        shadow = unpack(returned[g][: count[g]].astype(F32), returned[g][count[g] :].astype(F32), odd)
        shadow_out[0, rows[g]] = (shadow * active[rows[g]]).astype(BF16)

    for k in (1, 2, 3):
        sent(("S", "z", k), s_own)
        sent(("S", "x", k), s_x)
    sent(("S", "c"), s_c)
    for g in range(GROUPS):
        gather_end("a", g, got1[g])
        gather_end("b", g, got2[g])
        sent(("back", g), outgoing[g])
        for k in (1, 2, 3):
            sent(("Z", g, k), h_out[g].at[k - 1])
        for n in range(4):
            sent(("C", g, n), partial[g].at[0])
        for j in range(2):
            sent(("F", g, j), hop[g].at[0])
            for part in range(2):
                sent(("G", g, j, part), hop[g].at[0])


def shards(sections, act_in, grad_in, weight, gain, preempted):
    _, T, F = act_in.shape
    D = weight.shape[2]
    C = 4 * F
    anywhere = pl.BlockSpec(memory_space=pl.ANY)
    shape = jax.ShapeDtypeStruct
    copies = len(COPIES)
    count = (SPLIT[0], T - SPLIT[0])
    folded = [n + n // 2 for n in count]
    results = (
        shape((1, T, F), BF16),
        shape((1, T, F), BF16),
        shape((1, T, F), BF16),
        shape((1, F), F32),
        shape((1, F, D), BF16),
    )

    def blocks(*lead, extra=(0, 0)):
        return tuple(pltpu.VMEM((*lead, m + e, LANES), BF16) for m, e in zip(folded, extra))

    results = pl.pallas_call(
        functools.partial(kernel, sections, float(D)),
        out_shape=results,
        in_specs=[anywhere] * 5,
        out_specs=(pl.BlockSpec(memory_space=pltpu.VMEM),) * 5,
        scratch_shapes=[
            pltpu.VMEM((1, T, F), BF16),
            pltpu.VMEM((1, T, F), BF16),
            pltpu.VMEM((1, F), BF16),
            pltpu.VMEM((1, T), jnp.int32),
            pltpu.VMEM((8, F, C), BF16),
            pltpu.VMEM((8, F + PAD, C), BF16),
            pltpu.VMEM((8, PAD + T, C), BF16),
            pltpu.VMEM((max(count), C), BF16),
            pltpu.VMEM((8, 8, C), F32),
            blocks(8, 4, extra=(PAD, 0)),
            blocks(8, 4),
            pltpu.VMEM((PAD + T, F + PAD), F32),
            pltpu.VMEM((T, LANES), F32),
            blocks(),
            blocks(),
            blocks(8, 4),
            blocks(4, 4),
            blocks(2, 2),
            blocks(2, 4),
            blocks(3),
            blocks(3),
            pltpu.VMEM((8, 256), F32),
            pltpu.VMEM((3, 8, 256), F32),
            pltpu.VMEM((8, 256), F32),
            pltpu.VMEM((3, 8, 256), F32),
            pltpu.VMEM((8, 256), F32),
            pltpu.VMEM((8, 256), F32),
            pltpu.VMEM((8, F), F32),
            pltpu.VMEM((T, LANES), F32),
            pltpu.VMEM((T, LANES), F32),
            pltpu.VMEM((T, F), BF16),
            pltpu.VMEM((F, T), BF16),
            pltpu.SemaphoreType.DMA((copies,)),
            pltpu.SemaphoreType.DMA((copies,)),
            pltpu.SemaphoreType.DMA((8,)),
            pltpu.SemaphoreType.DMA((4,)),
        ],
        compiler_params=pltpu.CompilerParams(
            collective_id=0, has_side_effects=True, vmem_limit_bytes=48 * 1024 * 1024
        ),
    )(*[pltpu.with_memory_space_constraint(a, pltpu.HBM) for a in (act_in, grad_in, gain, preempted, weight)])
    next_input, shadow, input_grad, gain_grad, weight_grad = results
    return next_input, shadow, input_grad, weight_grad, gain_grad


def solution(mesh):
    return jax.shard_map(
        functools.partial(shards, mesh.shape["section"]),
        mesh=mesh,
        in_specs=(
            P("section", None, ("dp", "mp")),
            P("section", None, ("dp", "mp")),
            P("section", ("dp", "mp"), None),
            P("section", ("dp", "mp")),
            P("section", None),
        ),
        out_specs=(
            P("section", None, ("dp", "mp")),
            P("section", None, ("dp", "mp")),
            P("section", None, ("dp", "mp")),
            P("section", ("dp", "mp"), None),
            P("section", ("dp", "mp")),
        ),
        check_vma=False,
    )
```

```python
import functools

import jax
import jax.numpy as jnp
from jax import lax
from jax.experimental import pallas as pl
from jax.experimental.pallas import tpu as pltpu
from jax.sharding import PartitionSpec as P

EPS = 1e-05
MESH = pl.DeviceIdType.MESH
F32 = jnp.float32
BF16 = jnp.bfloat16
LANES = 128
HALF = 64
PAD = 16

NT = (((1,), (1,)), ((), ()))
NN = (((1,), (0,)), ((), ()))


def dot(a, b, dims):
    return lax.dot_general(a, b, dims, preferred_element_type=F32)


def low_lanes(rows):
    return lax.broadcasted_iota(jnp.int32, (rows, LANES), 1) < HALF


def half_turn(value):
    return pltpu.roll(value, HALF, 1)


def split_tiles(value):
    tail = value[:, LANES:]
    return value[:, :LANES], jnp.concatenate([tail, tail], axis=1)


def main_and_rest(value, odd):
    first, tail = split_tiles(value)
    low = low_lanes(value.shape[0])
    turned = half_turn(first)
    main = jnp.where(odd, jnp.where(low, turned, tail), first)
    rest = jnp.where(odd, jnp.where(low, first, turned), tail)
    return main, rest


def pack(value, odd):
    half = value.shape[0] // 2
    main, rest = main_and_rest(value, odd)
    here = low_lanes(half) != odd
    return main, jnp.where(here, rest[:half], rest[half:])


def unpack(main, folded, odd):
    half = folded.shape[0]
    here = low_lanes(half) != odd
    turned = half_turn(folded)
    rest = jnp.concatenate([jnp.where(here, folded, turned), jnp.where(here, turned, folded)], axis=0)
    main_turned = half_turn(main)
    first = jnp.where(odd, jnp.where(low_lanes(main.shape[0]), rest, main_turned), main)
    tail = jnp.where(odd, main_turned, rest)
    return jnp.concatenate([first, tail[:, :HALF]], axis=1)


def gelu_parts(p):
    k = 0.7978845608028654
    t = jnp.tanh(k * (p + 0.044715 * (p * p * p)))
    return t, k * (1.0 + (3.0 * 0.044715) * (p * p))


def eye(rows, columns):
    return lax.broadcasted_iota(jnp.int32, (rows, columns), 0) == lax.broadcasted_iota(
        jnp.int32, (rows, columns), 1
    )


def as_column(row):
    n = row.shape[1]
    return jnp.sum(jnp.where(eye(n, n), jnp.broadcast_to(row, (n, n)), 0.0), axis=1, keepdims=True)


def as_row(column, width, start):
    n = column.shape[0]
    here = lax.broadcasted_iota(jnp.int32, (n, width), 0) + start == lax.broadcasted_iota(jnp.int32, (n, width), 1)
    return jnp.sum(jnp.where(here, jnp.broadcast_to(column, (n, width)), 0.0), axis=0, keepdims=True)


GROUPS = 2
SPLIT = (96, 64)
DIRECT = {"a": (0, 3), "b": (3,)}
COPIES = (
    [(tag, g, "z", k) for tag in "ab" for g in range(GROUPS) for k in (1, 2, 3)]
    + [(tag, g, kind, k) for tag in "ab" for g in range(GROUPS) for kind in "+-s" for k in range(4)]
    + [(tag, g, "f", k) for tag in "ab" for g in range(GROUPS) for k in range(4)]
    + [(name, g) for name in ("next", "back") for g in range(GROUPS)]
    + [("S", "z", k) for k in (1, 2, 3)]
    + [("S", "x", k) for k in (1, 2, 3)]
    + [("S", "c")]
    + [("C", g, j) for g in range(GROUPS) for j in range(4)]
    + [("F", g, j) for g in range(GROUPS) for j in range(2)]
    + [("G", g, j, part) for g in range(GROUPS) for j in range(2) for part in range(2)]
    + [("Z", g, k) for g in range(GROUPS) for k in (1, 2, 3)]
)
COPY_ID = {name: index for index, name in enumerate(COPIES)}


def kernel(
    sections,
    features,
    act,
    grad,
    gain,
    preempted,
    weight,
    rows_out,
    gain_grad_out,
    weight_grad_out,
    act_v,
    grad_v,
    gain_v,
    preempted_v,
    wv,
    wp,
    xs,
    xs2,
    gains,
    got1,
    got2,
    acc,
    squares,
    outgoing,
    returned,
    partial,
    from_sib,
    hop,
    g_in,
    h_out,
    z_in,
    s_own,
    s_z,
    s_x,
    s_xr,
    s_c,
    s_cr,
    sums_s,
    mean_s,
    inv_s,
    dpre_s,
    dpre_t,
    held,
    hat_s,
    send_sem,
    recv_sem,
    w_sem,
    in_sem,
):
    T, F = act.shape[1], act.shape[2]
    C = 4 * F
    count = [SPLIT[0], T - SPLIT[0]]
    start = [0, SPLIT[0]]
    rows = [slice(start[g], start[g] + count[g]) for g in range(GROUPS)]
    folded = [n + n // 2 for n in count]
    section, dp, z = lax.axis_index("section"), lax.axis_index("dp"), lax.axis_index("mp")
    core = dp % 2
    sib = dp + 1 - 2 * core
    odd = (z % 2) == 1

    def near(c, step):
        return (c + 2 * step + 8) % 8

    up, down, far = near(dp, 1), near(dp, -1), near(dp, 2)
    to_up, to_down, to_far, to_sib = {"dp": up}, {"dp": down}, {"dp": far}, {"dp": sib}
    to_next = {"section": (section + 1) % sections}
    to_back = {"section": (section + sections - 1) % sections}

    def to_z(k):
        return {"mp": (z + k) % 4}

    def nth(k):
        if k == 1:
            return jnp.where(z % 2 == 0, 3, 1)
        if k == 2:
            return jnp.where(z == 1, 3, jnp.where(z == 2, 1, 2))
        if k == 3:
            return jnp.where(z == 0, 1, jnp.where(z == 3, 3, 2))
        return 0

    def zk(k):
        return (z + 4 - nth(k)) % 4

    def rc(name, src, dst, device, offset=0):
        n = COPY_ID[name] + offset
        return pltpu.make_async_remote_copy(
            src_ref=src,
            dst_ref=dst,
            send_sem=send_sem.at[n],
            recv_sem=recv_sem.at[n],
            device_id=device,
            device_id_type=MESH,
        )

    def send(name, src, dst, device):
        rc(name, src, dst, device).start()

    def arrive(name, dst, offset=0):
        rc(name, dst, dst, to_sib, offset).wait_recv()

    def sent(name, src):
        rc(name, src, src, to_sib).wait_send()

    small = [
        pltpu.make_async_copy(src, dst, in_sem.at[n])
        for n, (src, dst) in enumerate(
            ((act, act_v), (gain, gain_v), (grad, grad_v), (preempted, preempted_v))
        )
    ]

    def weight_copy(c):
        return pltpu.make_async_copy(weight.at[0, :, pl.ds(c * C, C)], wv.at[c], w_sem.at[c])

    for copy in small:
        copy.start()
    barrier = pltpu.get_barrier_semaphore()
    partners = [to_z(1), to_z(2), to_z(3), to_up, to_down, to_far, to_sib, to_next, to_back]
    for device in partners:
        pl.semaphore_signal(barrier, inc=1, device_id=device, device_id_type=MESH)
    for c in range(8):
        weight_copy(c).start()

    small[0].wait()
    small[1].wait()
    x_own = act_v[0].astype(F32)

    def put(block, g, value):
        main, fold = pack(value, odd)
        block[: count[g]] = main.astype(BF16)
        block[count[g] : folded[g]] = fold.astype(BF16)

    for g in range(GROUPS):
        put(got1[g].at[dp, z], g, x_own[rows[g]])
    gain_row = gain_v[...].astype(F32)
    g_main, g_rest = main_and_rest(jnp.broadcast_to(gain_row, (PAD, F)), odd)
    first_row = lax.broadcasted_iota(jnp.int32, (PAD, LANES), 0) == 0
    got1[0][dp, z, folded[0] :] = jnp.where(first_row, g_main, g_rest).astype(BF16)
    pl.semaphore_wait(barrier, len(partners))

    def own_to_z(tag, g, got):
        own = got.at[dp, z]
        for k in (1, 2, 3):
            send((tag, g, "z", k), own, own, to_z(k))

    def own_to_x(tag, g, got):
        own = got.at[dp, z]
        send((tag, g, "+", 0), own, own, to_up)
        send((tag, g, "-", 0), own, own, to_down)
        if 0 in DIRECT[tag]:
            send((tag, g, "f", 0), own, own, to_far)

    def from_z(tag, g, got, k):
        block = got.at[dp, zk(k)]
        arrive((tag, g, "z", 1), block, nth(k) - 1)
        send((tag, g, "+", k), block, block, to_up)
        send((tag, g, "-", k), block, block, to_down)
        if k in DIRECT[tag]:
            send((tag, g, "f", k), block, block, to_far)
        if k == 3:
            send((tag, g, "s", 0), got.at[dp], got.at[dp], to_sib)

    def from_x(tag, g, got, k):
        a, b = got.at[down, zk(k)], got.at[up, zk(k)]
        arrive((tag, g, "+", k), a)
        arrive((tag, g, "-", k), b)
        if k == 3:
            send((tag, g, "s", 1), got.at[down], got.at[down], to_sib)
            send((tag, g, "s", 2), got.at[up], got.at[up], to_sib)
        if k in DIRECT[tag]:
            pass
        elif (k + g) % 2 == 0:
            send((tag, g, "f", k), a, a, to_up)
        else:
            send((tag, g, "f", k), b, b, to_down)

    def from_far(tag, g, got):
        for k in range(4):
            arrive((tag, g, "f", k), got.at[far, zk(k)])
        send((tag, g, "s", 3), got.at[far], got.at[far], to_sib)

    def from_sib_core(tag, g, got, j):
        arrive((tag, g, "s", j), got.at[near(sib, (0, -1, 1, 2)[j])])

    def gather_end(tag, g, got):
        for k in range(4):
            if k:
                sent((tag, g, "z", k), got.at[0, 0])
            for kind in "+-f":
                sent((tag, g, kind, k), got.at[0, 0])
            sent((tag, g, "s", k), got.at[0])

    def chunk_of(i):
        step = jnp.where(i < 2, 0, jnp.where(i > 5, 2, jnp.where(i % 2 == 0, 3, 1)))
        flip = jnp.where((i == 1) | (i == 4) | (i == 5) | (i == 7), 1, 0)
        mine = (dp + 2 * step) % 8
        return mine + flip * (1 - 2 * core)

    def steps(work, events):
        def body(i, carry):
            for n in sorted(events):

                @pl.when(i == n)
                def _():
                    for action, *arguments in events[n]:
                        action(*arguments)

            work(i)
            return carry

        lax.fori_loop(0, 8, body, 0)

    def gather_events(tag, got, extra):
        def z(g, k):
            return (from_z, tag, g, got[g], k)

        def x(g, k):
            return (from_x, tag, g, got[g], k)

        def s(g, j):
            return (from_sib_core, tag, g, got[g], j)

        def f(g):
            return (from_far, tag, g, got[g])

        first = {
            0: [z(0, 1), (own_to_z, tag, 1, got[1]), x(0, 0), z(0, 2), z(0, 3)],
            1: [x(0, 1), z(1, 1), s(0, 0)],
            2: [x(0, 2), z(1, 2), x(1, 0), x(0, 3), z(1, 3)],
            4: [x(1, 1), s(0, 1)],
            5: [x(1, 2), s(0, 2)],
            6: [f(0)],
            7: [s(0, 3)],
        }
        second = {
            0: [x(1, 3)],
            1: [s(1, 0)],
            3: [f(1)],
            4: [s(1, 1)],
            5: [s(1, 2)],
            7: [s(1, 3)],
        }
        for (g, n), actions in extra.items():
            events = (first, second)[g]
            events[n] = events.get(n, []) + actions
        return first, second

    own_to_z("a", 0, got1[0])
    for g in range(GROUPS):
        own_to_x("a", g, got1[g])

    ones = jnp.ones((PAD, C), BF16)

    def fill(c, carry):
        xs[c, :PAD] = ones
        wp[c, F:] = ones
        return carry

    lax.fori_loop(0, 8, fill, 0)

    low = [low_lanes(n // 2) for n in count]

    def unfold_chunk(got, g, c, keep):
        n, m = count[g], folded[g]
        total = squares[rows[g]]
        for p in range(2):
            r0 = got[c, 2 * p, n:m].astype(F32)
            r1 = got[c, 2 * p + 1, n:m].astype(F32)
            middle = jnp.concatenate(
                [jnp.where(low[g], r0, r1), half_turn(jnp.where(low[g], r1, r0))], axis=0
            )
            t0 = got[c, 2 * p, :n]
            t2 = got[c, 2 * p + 1, :n]
            keep(3 * p, t0)
            keep(3 * p + 1, middle.astype(BF16))
            keep(3 * p + 2, t2)
            t0, t2 = t0.astype(F32), t2.astype(F32)
            total = total + (t0 * t0 + middle * middle + t2 * t2)
        squares[rows[g]] = total

    spot = [slice(PAD + start[g], PAD + start[g] + count[g]) for g in range(GROUPS)]
    fed = [slice(0, PAD + count[0]), spot[1]]

    def first_layer(g):
        def work(i):
            c = chunk_of(i)
            if g == 0:
                row_low = low_lanes(1)
                for p in range(2):
                    g0 = got1[0][c, 2 * p, folded[0] :].astype(F32)
                    g1 = got1[0][c, 2 * p + 1, folded[0] :].astype(F32)
                    for j, row in enumerate((g0[0:1], jnp.where(row_low, g0[1:2], g1[1:2]), g1[0:1])):
                        gains[c, :, (3 * p + j) * LANES : (3 * p + j + 1) * LANES] = jnp.broadcast_to(
                            row, (8, LANES)
                        )
                wp[c, :F] = (wv[c].astype(F32) * gains[c, 0:1]).astype(BF16)

            def keep(t, value):
                xs[c, spot[g], t * LANES : (t + 1) * LANES] = value

            unfold_chunk(got1[g], g, c, keep)
            acc[fed[g]] += dot(xs[c, fed[g]], wp[c], NT)

        return work

    def second_layer(g):
        def work(i):
            c = chunk_of(i)

            def keep(t, value):
                xs2[: count[g], t * LANES : (t + 1) * LANES] = value

            unfold_chunk(got2[g], g, c, keep)
            acc[spot[g]] += dot(xs2[: count[g]], wp[c], NT)

        return work

    def row_statistics(g):
        mean = acc[spot[g], F : F + 1] / features
        variance = jnp.sum(squares[rows[g]], axis=1, keepdims=True) / features - mean * mean
        return mean, lax.rsqrt(variance + EPS)

    width = s_own.shape[1]
    row_is_0 = lax.broadcasted_iota(jnp.int32, (8, width), 0) == 0

    def finish_first(g):
        mean, inv_std = row_statistics(g)
        if g == 0:
            sums_s[...] = acc[0:8, :F]
        weight_sums = sums_s[0:1]
        preact = inv_std * (acc[spot[g], :F] - mean * weight_sums)
        t, slope = gelu_parts(preact)
        x = act_v[0, rows[g]].astype(F32)
        layer_out = x + 0.5 * preact * (1.0 + t)
        put(outgoing[g], g, layer_out.astype(BF16).astype(F32))
        send(("next", g), outgoing[g], got2[g].at[dp, z], to_next)

        derivative = 0.5 * (1.0 + t) + 0.5 * preact * (1.0 - t * t) * slope
        dpre = (grad_v[0, rows[g]].astype(F32) * derivative).astype(BF16)
        dpre_s[rows[g]] = dpre
        dpre_f = dpre.astype(F32)
        mean_s[rows[g]] = jnp.broadcast_to(mean, (count[g], LANES))
        inv_s[rows[g]] = jnp.broadcast_to(inv_std, (count[g], LANES))
        sum_grad = as_row(jnp.sum(dpre_f * weight_sums, axis=1, keepdims=True), width, start[g])
        sum_proj = as_row(jnp.sum(dpre_f * preact, axis=1, keepdims=True), width, start[g])
        both = jnp.where(row_is_0, sum_grad, sum_proj)
        s_own[...] = both if g == 0 else s_own[...] + both

    def finish_second(g):
        mean, inv_std = row_statistics(g)
        preact = inv_std * (acc[spot[g], :F] - mean * sums_s[0:1])
        t, _ = gelu_parts(preact)
        own = got2[g].at[dp, z]
        x = unpack(own[: count[g]].astype(F32), own[count[g] :].astype(F32), odd)
        redundant = (x + 0.5 * preact * (1.0 + t)).astype(BF16).astype(F32)
        sent(("next", g), outgoing[g])
        put(outgoing[g], g, redundant)
        send(("back", g), outgoing[g], returned[g], to_back)
        rows_out[0, rows[g]] = jnp.where(section > 0, x, 0.0).astype(BF16)

    def x_of(j):
        return (dp // 2 + jnp.where(j == 0, 2, jnp.where(j == 1, 1, jnp.where(j == 2, 3, 0)))) % 4

    def partial_sums(g):
        n, h = count[g], count[g] // 2

        def body(i, carry):
            j = i % 4
            theirs = i < 4
            x = x_of(j)
            c = 2 * x + jnp.where(theirs, 1 - core, core)
            product = dot(dpre_s[rows[g]], wv[c], NN)
            for p in range(2):
                tile = [product[:, (3 * p + q) * LANES : (3 * p + q + 1) * LANES] for q in range(3)]
                top, bottom = tile[1][:h], half_turn(tile[1][h:])
                partial[g][c, 2 * p, :n] = tile[0].astype(BF16)
                partial[g][c, 2 * p, n:] = jnp.where(low[g], top, bottom).astype(BF16)
                partial[g][c, 2 * p + 1, :n] = tile[2].astype(BF16)
                partial[g][c, 2 * p + 1, n:] = jnp.where(low[g], bottom, top).astype(BF16)
            for m in range(4):

                @pl.when(i == m)
                def _():
                    send(("C", g, m), partial[g].at[c], from_sib[g].at[x], to_sib)

            return carry

        lax.fori_loop(0, 8, body, 0)

    def fold_in(g, c, source, index, first, blocks):
        for b in range(blocks):
            partial[g][c, first + b] = (
                partial[g][c, first + b].astype(F32) + source[index, b].astype(F32)
            ).astype(BF16)

    def from_sibling(g, n):
        x = x_of(n)
        arrive(("C", g, n), from_sib[g].at[x])
        fold_in(g, 2 * x + core, from_sib[g], x, 0, 4)

    def reduce_begin(g):
        from_sibling(g, 0)
        send(("F", g, 0), partial[g].at[far, 0:2], hop[g].at[0], to_up)
        send(("F", g, 1), partial[g].at[far, 2:4], hop[g].at[1], to_down)
        from_sibling(g, 1)
        send(("G", g, 0, 0), partial[g].at[up, 2:4], g_in[g].at[0, 2:4], to_up)
        from_sibling(g, 2)
        send(("G", g, 1, 0), partial[g].at[down, 0:2], g_in[g].at[1, 0:2], to_down)
        from_sibling(g, 3)

    def reduce_hop(g):
        arrive(("F", g, 0), hop[g].at[0])
        fold_in(g, up, hop[g], 0, 0, 2)
        send(("G", g, 0, 1), partial[g].at[up, 0:2], g_in[g].at[0, 0:2], to_up)
        arrive(("F", g, 1), hop[g].at[1])
        fold_in(g, down, hop[g], 1, 2, 2)
        send(("G", g, 1, 1), partial[g].at[down, 2:4], g_in[g].at[1, 2:4], to_down)

    def sum_x(g, b):
        return partial[g][dp, b].astype(F32) + (g_in[g][0, b].astype(F32) + g_in[g][1, b].astype(F32))

    def reduce_z(g):
        arrive(("G", g, 0, 0), g_in[g].at[0, 2:4])
        arrive(("G", g, 1, 0), g_in[g].at[1, 0:2])
        arrive(("G", g, 0, 1), g_in[g].at[0, 0:2])
        arrive(("G", g, 1, 1), g_in[g].at[1, 2:4])
        for k in (1, 2, 3):
            h_out[g][k - 1] = sum_x(g, (z + k) % 4).astype(BF16)
            send(("Z", g, k), h_out[g].at[k - 1], z_in[g].at[k - 1], to_z(k))

    def reduce_end(g):
        total = sum_x(g, z)
        for k in (1, 2, 3):
            arrive(("Z", g, k), z_in[g].at[k - 1])
            total = total + z_in[g][k - 1].astype(F32)
        return unpack(total[: count[g]], total[count[g] :], odd)

    def sums_x():
        for k in (1, 2, 3):
            arrive(("S", "z", k), s_z.at[k - 1])
        s_x[...] = s_own[...] + (s_z[0] + s_z[1] + s_z[2])
        for k in (1, 2, 3):
            send(("S", "x", k), s_x, s_xr.at[k - 1], {"dp": near(dp, k)})

    def sums_core():
        for k in (1, 2, 3):
            arrive(("S", "x", k), s_xr.at[k - 1])
        s_c[...] = s_x[...] + (s_xr[0] + s_xr[1] + s_xr[2])
        send(("S", "c"), s_c, s_cr, to_sib)

    def weight_grad_chunk(c, carry):
        x = xs[c, PAD:].astype(F32)
        normed = ((x - mean_s[:, 0:1]) * inv_s[:, 0:1] * gains[c, 0:1]).astype(BF16)
        weight_grad_out[0, :, pl.ds(pl.multiple_of(c * C, C), C)] = dot(dpre_t[...], normed, NN).astype(BF16)
        return carry

    acc[...] = jnp.zeros_like(acc)
    squares[...] = jnp.zeros_like(squares)
    for c in range(8):
        weight_copy(c).wait()
    small[2].wait()
    small[3].wait()
    events = gather_events("a", got1, {(1, 2): [(reduce_begin, 0)]})
    steps(first_layer(0), events[0])
    finish_first(0)
    partial_sums(0)
    steps(first_layer(1), events[1])
    finish_first(1)
    for k in (1, 2, 3):
        send(("S", "z", k), s_own, s_z.at[k - 1], to_z(k))
    partial_sums(1)
    acc[...] = jnp.zeros_like(acc)
    squares[...] = jnp.zeros_like(squares)
    reduce_begin(1)

    arrive(("next", 0), got2[0].at[dp, z])
    own_to_z("b", 0, got2[0])
    own_to_x("b", 0, got2[0])
    dpre_t[...] = dot(jnp.where(eye(F, F), 1.0, 0.0).astype(BF16), dpre_s[...], NT).astype(BF16)
    reduce_hop(0)
    lax.fori_loop(0, 8, weight_grad_chunk, 0)
    arrive(("next", 1), got2[1].at[dp, z])
    own_to_x("b", 1, got2[1])
    reduce_hop(1)
    sums_x()
    events = gather_events(
        "b",
        got2,
        {(0, 1): [(reduce_z, 0)], (1, 0): [(reduce_z, 1)], (1, 4): [(sums_core,)]},
    )
    steps(second_layer(0), events[0])
    finish_second(0)
    steps(second_layer(1), events[1])
    finish_second(1)

    active = as_column(preempted_v[...].astype(F32)) * jnp.where(section < sections - 1, 1.0, 0.0)
    arrive(("S", "c"), s_cr)
    sums = (s_c[...] + s_cr[...])[:, :T] / features
    mean_grad = as_column(sums[0:1])
    mean_proj = as_column(sums[1:2])
    inv_std = inv_s[:, 0:1]
    x_hat = (act_v[0].astype(F32) - mean_s[:, 0:1]) * inv_std
    held[...] = grad_v[0].astype(F32) - inv_std * (mean_grad + x_hat * mean_proj)
    hat_s[...] = x_hat
    gain_grad = jnp.zeros((1, F), F32)
    for g in range(GROUPS):
        dnormed = reduce_end(g)
        gain_grad = gain_grad + jnp.sum(dnormed * hat_s[rows[g]], axis=0, keepdims=True)
        dhat = dnormed * gain_v[...].astype(F32)
        rows_out[2, rows[g]] = (held[rows[g]] + inv_s[rows[g], 0:1] * dhat).astype(BF16)
    gain_grad_out[...] = gain_grad

    for g in range(GROUPS):
        arrive(("back", g), returned[g])
        shadow = unpack(returned[g][: count[g]].astype(F32), returned[g][count[g] :].astype(F32), odd)
        rows_out[1, rows[g]] = (shadow * active[rows[g]]).astype(BF16)

    for k in (1, 2, 3):
        sent(("S", "z", k), s_own)
        sent(("S", "x", k), s_x)
    sent(("S", "c"), s_c)
    for g in range(GROUPS):
        gather_end("a", g, got1[g])
        gather_end("b", g, got2[g])
        sent(("back", g), outgoing[g])
        for k in (1, 2, 3):
            sent(("Z", g, k), h_out[g].at[k - 1])
        for n in range(4):
            sent(("C", g, n), partial[g].at[0])
        for j in range(2):
            sent(("F", g, j), hop[g].at[0])
            for part in range(2):
                sent(("G", g, j, part), hop[g].at[0])


def shards(sections, act_in, grad_in, weight, gain, preempted):
    _, T, F = act_in.shape
    D = weight.shape[2]
    C = 4 * F
    anywhere = pl.BlockSpec(memory_space=pl.ANY)
    shape = jax.ShapeDtypeStruct
    copies = len(COPIES)
    count = (SPLIT[0], T - SPLIT[0])
    folded = [n + n // 2 for n in count]
    results = (
        shape((3, T, F), BF16),
        shape((1, F), F32),
        shape((1, F, D), BF16),
    )

    def blocks(*lead, extra=(0, 0)):
        return tuple(pltpu.VMEM((*lead, m + e, LANES), BF16) for m, e in zip(folded, extra))

    results = pl.pallas_call(
        functools.partial(kernel, sections, float(D)),
        out_shape=results,
        in_specs=[anywhere] * 5,
        out_specs=(pl.BlockSpec(memory_space=pltpu.VMEM),) * 3,
        scratch_shapes=[
            pltpu.VMEM((1, T, F), BF16),
            pltpu.VMEM((1, T, F), BF16),
            pltpu.VMEM((1, F), BF16),
            pltpu.VMEM((1, T), jnp.int32),
            pltpu.VMEM((8, F, C), BF16),
            pltpu.VMEM((8, F + PAD, C), BF16),
            pltpu.VMEM((8, PAD + T, C), BF16),
            pltpu.VMEM((max(count), C), BF16),
            pltpu.VMEM((8, 8, C), F32),
            blocks(8, 4, extra=(PAD, 0)),
            blocks(8, 4),
            pltpu.VMEM((PAD + T, F + PAD), F32),
            pltpu.VMEM((T, LANES), F32),
            blocks(),
            blocks(),
            blocks(8, 4),
            blocks(4, 4),
            blocks(2, 2),
            blocks(2, 4),
            blocks(3),
            blocks(3),
            pltpu.VMEM((8, 256), F32),
            pltpu.VMEM((3, 8, 256), F32),
            pltpu.VMEM((8, 256), F32),
            pltpu.VMEM((3, 8, 256), F32),
            pltpu.VMEM((8, 256), F32),
            pltpu.VMEM((8, 256), F32),
            pltpu.VMEM((8, F), F32),
            pltpu.VMEM((T, LANES), F32),
            pltpu.VMEM((T, LANES), F32),
            pltpu.VMEM((T, F), BF16),
            pltpu.VMEM((F, T), BF16),
            pltpu.VMEM((T, F), F32),
            pltpu.VMEM((T, F), F32),
            pltpu.SemaphoreType.DMA((copies,)),
            pltpu.SemaphoreType.DMA((copies,)),
            pltpu.SemaphoreType.DMA((8,)),
            pltpu.SemaphoreType.DMA((4,)),
        ],
        compiler_params=pltpu.CompilerParams(
            collective_id=0, has_side_effects=True, vmem_limit_bytes=48 * 1024 * 1024
        ),
    )(*[pltpu.with_memory_space_constraint(a, pltpu.HBM) for a in (act_in, grad_in, gain, preempted, weight)])
    by_row, gain_grad, weight_grad = results
    next_input, shadow, input_grad = by_row[0:1], by_row[1:2], by_row[2:3]
    return next_input, shadow, input_grad, weight_grad, gain_grad


def solution(mesh):
    return jax.shard_map(
        functools.partial(shards, mesh.shape["section"]),
        mesh=mesh,
        in_specs=(
            P("section", None, ("dp", "mp")),
            P("section", None, ("dp", "mp")),
            P("section", ("dp", "mp"), None),
            P("section", ("dp", "mp")),
            P("section", None),
        ),
        out_specs=(
            P("section", None, ("dp", "mp")),
            P("section", None, ("dp", "mp")),
            P("section", None, ("dp", "mp")),
            P("section", ("dp", "mp"), None),
            P("section", ("dp", "mp")),
        ),
        check_vma=False,
    )
```

```python
import functools

import jax
import jax.numpy as jnp
from jax import lax
from jax.experimental import pallas as pl
from jax.experimental.pallas import tpu as pltpu
from jax.sharding import PartitionSpec as P

EPS = 1e-05
MESH = pl.DeviceIdType.MESH
F32 = jnp.float32
BF16 = jnp.bfloat16
LANES = 128
HALF = 64
PAD = 16

NT = (((1,), (1,)), ((), ()))
NN = (((1,), (0,)), ((), ()))


def dot(a, b, dims):
    return lax.dot_general(a, b, dims, preferred_element_type=F32)


def low_lanes(rows):
    return lax.broadcasted_iota(jnp.int32, (rows, LANES), 1) < HALF


def half_turn(value):
    return pltpu.roll(value, HALF, 1)


def split_tiles(value):
    tail = value[:, LANES:]
    return value[:, :LANES], jnp.concatenate([tail, tail], axis=1)


def main_and_rest(value, odd):
    first, tail = split_tiles(value)
    low = low_lanes(value.shape[0])
    turned = half_turn(first)
    main = jnp.where(odd, jnp.where(low, turned, tail), first)
    rest = jnp.where(odd, jnp.where(low, first, turned), tail)
    return main, rest


def pack(value, odd):
    half = value.shape[0] // 2
    main, rest = main_and_rest(value, odd)
    here = low_lanes(half) != odd
    return main, jnp.where(here, rest[:half], rest[half:])


def unpack(main, folded, odd):
    half = folded.shape[0]
    here = low_lanes(half) != odd
    turned = half_turn(folded)
    rest = jnp.concatenate([jnp.where(here, folded, turned), jnp.where(here, turned, folded)], axis=0)
    main_turned = half_turn(main)
    first = jnp.where(odd, jnp.where(low_lanes(main.shape[0]), rest, main_turned), main)
    tail = jnp.where(odd, main_turned, rest)
    return jnp.concatenate([first, tail[:, :HALF]], axis=1)


def gelu_parts(p):
    k = 0.7978845608028654
    t = jnp.tanh(k * (p + 0.044715 * (p * p * p)))
    return t, k * (1.0 + (3.0 * 0.044715) * (p * p))


def eye(rows, columns):
    return lax.broadcasted_iota(jnp.int32, (rows, columns), 0) == lax.broadcasted_iota(
        jnp.int32, (rows, columns), 1
    )


def as_column(row):
    n = row.shape[1]
    return jnp.sum(jnp.where(eye(n, n), jnp.broadcast_to(row, (n, n)), 0.0), axis=1, keepdims=True)


def as_row(column, width, start):
    n = column.shape[0]
    here = lax.broadcasted_iota(jnp.int32, (n, width), 0) + start == lax.broadcasted_iota(jnp.int32, (n, width), 1)
    return jnp.sum(jnp.where(here, jnp.broadcast_to(column, (n, width)), 0.0), axis=0, keepdims=True)


GROUPS = 2
SPLIT = (96, 64)
DIRECT = {"a": (0, 3), "b": (3,)}
COPIES = (
    [(tag, g, "z", k) for tag in "ab" for g in range(GROUPS) for k in (1, 2, 3)]
    + [(tag, g, kind, k) for tag in "ab" for g in range(GROUPS) for kind in "+-s" for k in range(4) if (kind, k) != ("s", 3)]
    + [(tag, g, kind, k) for tag in "ab" for g in range(GROUPS) for kind in "ft" for k in range(4)]
    + [(name, g) for name in ("next", "back") for g in range(GROUPS)]
    + [("S", "z", k) for k in (1, 2, 3)]
    + [("S", "x", k) for k in (1, 2, 3)]
    + [("S", "c")]
    + [("C", g, j) for g in range(GROUPS) for j in range(4)]
    + [("F", g, j) for g in range(GROUPS) for j in range(2)]
    + [("G", g, j, part) for g in range(GROUPS) for j in range(2) for part in range(2)]
    + [("Z", g, k) for g in range(GROUPS) for k in (1, 2, 3)]
)
COPY_ID = {name: index for index, name in enumerate(COPIES)}


def kernel(
    sections,
    features,
    act,
    grad,
    gain,
    preempted,
    weight,
    rows_out,
    gain_grad_out,
    weight_grad_out,
    act_v,
    grad_v,
    gain_v,
    preempted_v,
    wv,
    wp,
    xs,
    xs2,
    gains,
    got1,
    got2,
    acc,
    squares,
    outgoing,
    returned,
    partial,
    from_sib,
    hop,
    g_in,
    h_out,
    z_in,
    s_own,
    s_z,
    s_x,
    s_xr,
    s_c,
    s_cr,
    sums_s,
    mean_s,
    inv_s,
    dpre_s,
    dpre_t,
    held,
    hat_s,
    send_sem,
    recv_sem,
    w_sem,
    in_sem,
):
    T, F = act.shape[1], act.shape[2]
    C = 4 * F
    count = [SPLIT[0], T - SPLIT[0]]
    start = [0, SPLIT[0]]
    rows = [slice(start[g], start[g] + count[g]) for g in range(GROUPS)]
    folded = [n + n // 2 for n in count]
    section, dp, z = lax.axis_index("section"), lax.axis_index("dp"), lax.axis_index("mp")
    core = dp % 2
    sib = dp + 1 - 2 * core
    odd = (z % 2) == 1

    def near(c, step):
        return (c + 2 * step + 8) % 8

    up, down, far = near(dp, 1), near(dp, -1), near(dp, 2)
    to_up, to_down, to_far, to_sib = {"dp": up}, {"dp": down}, {"dp": far}, {"dp": sib}
    to_next = {"section": (section + 1) % sections}
    to_back = {"section": (section + sections - 1) % sections}

    def to_z(k):
        return {"mp": (z + k) % 4}

    def nth(k):
        if k == 1:
            return jnp.where(z % 2 == 0, 3, 1)
        if k == 2:
            return jnp.where(z == 1, 3, jnp.where(z == 2, 1, 2))
        if k == 3:
            return jnp.where(z == 0, 1, jnp.where(z == 3, 3, 2))
        return 0

    def zk(k):
        return (z + 4 - nth(k)) % 4

    def rc(name, src, dst, device, offset=0):
        n = COPY_ID[name] + offset
        return pltpu.make_async_remote_copy(
            src_ref=src,
            dst_ref=dst,
            send_sem=send_sem.at[n],
            recv_sem=recv_sem.at[n],
            device_id=device,
            device_id_type=MESH,
        )

    def send(name, src, dst, device):
        rc(name, src, dst, device).start()

    def arrive(name, dst, offset=0):
        rc(name, dst, dst, to_sib, offset).wait_recv()

    def sent(name, src):
        rc(name, src, src, to_sib).wait_send()

    small = [
        pltpu.make_async_copy(src, dst, in_sem.at[n])
        for n, (src, dst) in enumerate(
            ((act, act_v), (gain, gain_v), (grad, grad_v), (preempted, preempted_v))
        )
    ]

    def weight_copy(c):
        return pltpu.make_async_copy(weight.at[0, :, pl.ds(c * C, C)], wv.at[c], w_sem.at[c])

    barrier = pltpu.get_barrier_semaphore()
    partners = [to_z(1), to_z(2), to_z(3), to_up, to_down, to_far, to_sib, to_next, to_back]
    for device in partners:
        pl.semaphore_signal(barrier, inc=1, device_id=device, device_id_type=MESH)
    for copy in small:
        copy.start()
    for c in range(8):
        weight_copy(c).start()

    small[0].wait()
    small[1].wait()
    x_own = act_v[0].astype(F32)

    def put(block, g, value):
        main, fold = pack(value, odd)
        block[: count[g]] = main.astype(BF16)
        block[count[g] : folded[g]] = fold.astype(BF16)

    for g in range(GROUPS):
        put(got1[g].at[dp, z], g, x_own[rows[g]])
    gain_row = gain_v[...].astype(F32)
    g_main, g_rest = main_and_rest(jnp.broadcast_to(gain_row, (PAD, F)), odd)
    first_row = lax.broadcasted_iota(jnp.int32, (PAD, LANES), 0) == 0
    got1[0][dp, z, folded[0] :] = jnp.where(first_row, g_main, g_rest).astype(BF16)
    pl.semaphore_wait(barrier, len(partners))

    def own_to_z(tag, g, got):
        own = got.at[dp, z]
        for k in (1, 2, 3):
            send((tag, g, "z", k), own, own, to_z(k))

    def own_to_x(tag, g, got):
        own = got.at[dp, z]
        send((tag, g, "+", 0), own, own, to_up)
        send((tag, g, "-", 0), own, own, to_down)
        if 0 in DIRECT[tag]:
            send((tag, g, "f", 0), own, own, to_far)

    def from_z(tag, g, got, k):
        block = got.at[dp, zk(k)]
        arrive((tag, g, "z", 1), block, nth(k) - 1)
        send((tag, g, "+", k), block, block, to_up)
        send((tag, g, "-", k), block, block, to_down)
        if k in DIRECT[tag]:
            send((tag, g, "f", k), block, block, to_far)
        if k == 3:
            send((tag, g, "s", 0), got.at[dp], got.at[dp], to_sib)

    def from_x(tag, g, got, k):
        a, b = got.at[down, zk(k)], got.at[up, zk(k)]
        if (k + g) % 2 == 0:
            arrive((tag, g, "+", k), a)
            if k not in DIRECT[tag]:
                send((tag, g, "f", k), a, a, to_up)
            arrive((tag, g, "-", k), b)
        else:
            arrive((tag, g, "-", k), b)
            if k not in DIRECT[tag]:
                send((tag, g, "f", k), b, b, to_down)
            arrive((tag, g, "+", k), a)
        if k == 3:
            send((tag, g, "s", 1), got.at[down], got.at[down], to_sib)
            send((tag, g, "s", 2), got.at[up], got.at[up], to_sib)

    def from_far(tag, g, got):
        for k in range(4):
            block = got.at[far, zk(k)]
            arrive((tag, g, "f", k), block)
            send((tag, g, "t", k), block, block, to_sib)

    def from_sib_core(tag, g, got, j):
        c = near(sib, (0, -1, 1, 2)[j])
        if j < 3:
            arrive((tag, g, "s", j), got.at[c])
        else:
            for k in range(4):
                arrive((tag, g, "t", k), got.at[c, zk(k)])

    def gather_end(tag, g, got):
        for k in range(4):
            if k:
                sent((tag, g, "z", k), got.at[0, 0])
            for kind in "+-f":
                sent((tag, g, kind, k), got.at[0, 0])
            sent((tag, g, "t", k), got.at[0, 0])
            if k < 3:
                sent((tag, g, "s", k), got.at[0])

    def chunk_of(i):
        step = jnp.where(i < 2, 0, jnp.where(i > 5, 2, jnp.where(i % 2 == 0, 3, 1)))
        flip = jnp.where((i == 1) | (i == 4) | (i == 5) | (i == 7), 1, 0)
        mine = (dp + 2 * step) % 8
        return mine + flip * (1 - 2 * core)

    def steps(work, events):
        def body(i, carry):
            for n in sorted(events):

                @pl.when(i == n)
                def _():
                    for action, *arguments in events[n]:
                        action(*arguments)

            work(i)
            return carry

        lax.fori_loop(0, 8, body, 0)

    def gather_events(tag, got, extra):
        def z(g, k):
            return (from_z, tag, g, got[g], k)

        def x(g, k):
            return (from_x, tag, g, got[g], k)

        def s(g, j):
            return (from_sib_core, tag, g, got[g], j)

        def f(g):
            return (from_far, tag, g, got[g])

        first = {
            0: [z(0, 1), (own_to_z, tag, 1, got[1]), x(0, 0), z(0, 2), z(0, 3)],
            1: [x(0, 1), z(1, 1), s(0, 0)],
            2: [x(0, 2), z(1, 2), x(1, 0), x(0, 3), z(1, 3)],
            4: [x(1, 1), s(0, 1)],
            5: [x(1, 2), s(0, 2)],
            6: [f(0)],
            7: [s(0, 3)],
        }
        second = {
            0: [x(1, 3)],
            1: [s(1, 0)],
            3: [f(1)],
            4: [s(1, 1)],
            5: [s(1, 2)],
            7: [s(1, 3)],
        }
        for (g, n), actions in extra.items():
            events = (first, second)[g]
            events[n] = events.get(n, []) + actions
        return first, second

    own_to_z("a", 0, got1[0])
    for g in range(GROUPS):
        own_to_x("a", g, got1[g])

    ones = jnp.ones((PAD, C), BF16)

    def fill(c, carry):
        xs[c, :PAD] = ones
        wp[c, F:] = ones
        return carry

    lax.fori_loop(0, 8, fill, 0)

    low = [low_lanes(n // 2) for n in count]

    def unfold_chunk(got, g, c, keep):
        n, m = count[g], folded[g]
        total = squares[rows[g]]
        for p in range(2):
            r0 = got[c, 2 * p, n:m].astype(F32)
            r1 = got[c, 2 * p + 1, n:m].astype(F32)
            middle = jnp.concatenate(
                [jnp.where(low[g], r0, r1), half_turn(jnp.where(low[g], r1, r0))], axis=0
            )
            t0 = got[c, 2 * p, :n]
            t2 = got[c, 2 * p + 1, :n]
            keep(3 * p, t0)
            keep(3 * p + 1, middle.astype(BF16))
            keep(3 * p + 2, t2)
            t0, t2 = t0.astype(F32), t2.astype(F32)
            total = total + (t0 * t0 + middle * middle + t2 * t2)
        squares[rows[g]] = total

    spot = [slice(PAD + start[g], PAD + start[g] + count[g]) for g in range(GROUPS)]
    fed = [slice(0, PAD + count[0]), spot[1]]

    def first_layer(g):
        def work(i):
            c = chunk_of(i)
            if g == 0:
                row_low = low_lanes(1)
                for p in range(2):
                    g0 = got1[0][c, 2 * p, folded[0] :].astype(F32)
                    g1 = got1[0][c, 2 * p + 1, folded[0] :].astype(F32)
                    for j, row in enumerate((g0[0:1], jnp.where(row_low, g0[1:2], g1[1:2]), g1[0:1])):
                        gains[c, :, (3 * p + j) * LANES : (3 * p + j + 1) * LANES] = jnp.broadcast_to(
                            row, (8, LANES)
                        )
                wp[c, :F] = (wv[c].astype(F32) * gains[c, 0:1]).astype(BF16)

            def keep(t, value):
                xs[c, spot[g], t * LANES : (t + 1) * LANES] = value

            unfold_chunk(got1[g], g, c, keep)
            acc[fed[g]] += dot(xs[c, fed[g]], wp[c], NT)

        return work

    def second_layer(g):
        def work(i):
            c = chunk_of(i)

            def keep(t, value):
                xs2[: count[g], t * LANES : (t + 1) * LANES] = value

            unfold_chunk(got2[g], g, c, keep)
            acc[spot[g]] += dot(xs2[: count[g]], wp[c], NT)

        return work

    def row_statistics(g):
        mean = acc[spot[g], F : F + 1] / features
        variance = jnp.sum(squares[rows[g]], axis=1, keepdims=True) / features - mean * mean
        return mean, lax.rsqrt(variance + EPS)

    width = s_own.shape[1]
    row_is_0 = lax.broadcasted_iota(jnp.int32, (8, width), 0) == 0

    def finish_first(g):
        mean, inv_std = row_statistics(g)
        if g == 0:
            sums_s[...] = acc[0:8, :F]
        weight_sums = sums_s[0:1]
        preact = inv_std * (acc[spot[g], :F] - mean * weight_sums)
        t, slope = gelu_parts(preact)
        x = act_v[0, rows[g]].astype(F32)
        layer_out = x + 0.5 * preact * (1.0 + t)
        put(outgoing[g], g, layer_out.astype(BF16).astype(F32))
        send(("next", g), outgoing[g], got2[g].at[dp, z], to_next)

        derivative = 0.5 * (1.0 + t) + 0.5 * preact * (1.0 - t * t) * slope
        dpre = (grad_v[0, rows[g]].astype(F32) * derivative).astype(BF16)
        dpre_s[rows[g]] = dpre
        dpre_f = dpre.astype(F32)
        mean_s[rows[g]] = jnp.broadcast_to(mean, (count[g], LANES))
        inv_s[rows[g]] = jnp.broadcast_to(inv_std, (count[g], LANES))
        sum_grad = as_row(jnp.sum(dpre_f * weight_sums, axis=1, keepdims=True), width, start[g])
        sum_proj = as_row(jnp.sum(dpre_f * preact, axis=1, keepdims=True), width, start[g])
        both = jnp.where(row_is_0, sum_grad, sum_proj)
        s_own[...] = both if g == 0 else s_own[...] + both

    def finish_second(g):
        mean, inv_std = row_statistics(g)
        preact = inv_std * (acc[spot[g], :F] - mean * sums_s[0:1])
        t, _ = gelu_parts(preact)
        redundant = (hat_s[rows[g]] + 0.5 * preact * (1.0 + t)).astype(BF16).astype(F32)
        put(outgoing[g], g, redundant)
        send(("back", g), outgoing[g], returned[g], to_back)

    def predecessor(g):
        sent(("next", g), outgoing[g])
        own = got2[g].at[dp, z]
        x = unpack(own[: count[g]].astype(F32), own[count[g] :].astype(F32), odd)
        hat_s[rows[g]] = x
        rows_out[0, rows[g]] = jnp.where(section > 0, x, 0.0).astype(BF16)

    def x_of(j):
        return (dp // 2 + jnp.where(j == 0, 2, jnp.where(j == 1, 1, jnp.where(j == 2, 3, 0)))) % 4

    def partial_sums(g):
        n, h = count[g], count[g] // 2

        def body(i, carry):
            j = i % 4
            theirs = i < 4
            x = x_of(j)
            c = 2 * x + jnp.where(theirs, 1 - core, core)
            product = dot(dpre_s[rows[g]], wv[c], NN)
            for p in range(2):
                tile = [product[:, (3 * p + q) * LANES : (3 * p + q + 1) * LANES] for q in range(3)]
                top, bottom = tile[1][:h], half_turn(tile[1][h:])
                partial[g][c, 2 * p, :n] = tile[0].astype(BF16)
                partial[g][c, 2 * p, n:] = jnp.where(low[g], top, bottom).astype(BF16)
                partial[g][c, 2 * p + 1, :n] = tile[2].astype(BF16)
                partial[g][c, 2 * p + 1, n:] = jnp.where(low[g], bottom, top).astype(BF16)
            for m in range(4):

                @pl.when(i == m)
                def _():
                    send(("C", g, m), partial[g].at[c], from_sib[g].at[x], to_sib)

            return carry

        lax.fori_loop(0, 8, body, 0)

    def fold_in(g, c, source, index, first, blocks):
        for b in range(blocks):
            partial[g][c, first + b] = (
                partial[g][c, first + b].astype(F32) + source[index, b].astype(F32)
            ).astype(BF16)

    def from_sibling(g, n):
        x = x_of(n)
        arrive(("C", g, n), from_sib[g].at[x])
        fold_in(g, 2 * x + core, from_sib[g], x, 0, 4)

    def reduce_begin(g):
        from_sibling(g, 0)
        send(("F", g, 0), partial[g].at[far, 0:2], hop[g].at[0], to_up)
        send(("F", g, 1), partial[g].at[far, 2:4], hop[g].at[1], to_down)
        from_sibling(g, 1)
        send(("G", g, 0, 0), partial[g].at[up, 2:4], g_in[g].at[0, 2:4], to_up)
        from_sibling(g, 2)
        send(("G", g, 1, 0), partial[g].at[down, 0:2], g_in[g].at[1, 0:2], to_down)
        from_sibling(g, 3)

    def reduce_hop(g):
        arrive(("F", g, 0), hop[g].at[0])
        fold_in(g, up, hop[g], 0, 0, 2)
        send(("G", g, 0, 1), partial[g].at[up, 0:2], g_in[g].at[0, 0:2], to_up)
        arrive(("F", g, 1), hop[g].at[1])
        fold_in(g, down, hop[g], 1, 2, 2)
        send(("G", g, 1, 1), partial[g].at[down, 2:4], g_in[g].at[1, 2:4], to_down)

    def sum_x(g, b):
        return partial[g][dp, b].astype(F32) + (g_in[g][0, b].astype(F32) + g_in[g][1, b].astype(F32))

    def reduce_z(g):
        arrive(("G", g, 0, 0), g_in[g].at[0, 2:4])
        arrive(("G", g, 1, 0), g_in[g].at[1, 0:2])
        arrive(("G", g, 0, 1), g_in[g].at[0, 0:2])
        arrive(("G", g, 1, 1), g_in[g].at[1, 2:4])
        for k in (1, 2, 3):
            h_out[g][k - 1] = sum_x(g, (z + k) % 4).astype(BF16)
            send(("Z", g, k), h_out[g].at[k - 1], z_in[g].at[k - 1], to_z(k))

    def reduce_end(g):
        total = sum_x(g, z)
        for k in (1, 2, 3):
            arrive(("Z", g, k), z_in[g].at[k - 1])
            total = total + z_in[g][k - 1].astype(F32)
        return unpack(total[: count[g]], total[count[g] :], odd)

    def sums_x():
        for k in (1, 2, 3):
            arrive(("S", "z", k), s_z.at[k - 1])
        s_x[...] = s_own[...] + (s_z[0] + s_z[1] + s_z[2])
        for k in (1, 2, 3):
            send(("S", "x", k), s_x, s_xr.at[k - 1], {"dp": near(dp, k)})

    def sums_core():
        for k in (1, 2, 3):
            arrive(("S", "x", k), s_xr.at[k - 1])
        s_c[...] = s_x[...] + (s_xr[0] + s_xr[1] + s_xr[2])
        send(("S", "c"), s_c, s_cr, to_sib)

    def weight_grad_chunk(c, carry):
        x = xs[c, PAD:].astype(F32)
        normed = ((x - mean_s[:, 0:1]) * inv_s[:, 0:1] * gains[c, 0:1]).astype(BF16)
        weight_grad_out[0, :, pl.ds(pl.multiple_of(c * C, C), C)] = dot(dpre_t[...], normed, NN).astype(BF16)
        return carry

    acc[...] = jnp.zeros_like(acc)
    squares[...] = jnp.zeros_like(squares)
    for c in range(8):
        weight_copy(c).wait()
    small[2].wait()
    small[3].wait()
    events = gather_events("a", got1, {(1, 2): [(reduce_begin, 0)]})
    steps(first_layer(0), events[0])
    finish_first(0)
    partial_sums(0)
    steps(first_layer(1), events[1])
    finish_first(1)
    for k in (1, 2, 3):
        send(("S", "z", k), s_own, s_z.at[k - 1], to_z(k))
    partial_sums(1)
    acc[...] = jnp.zeros_like(acc)
    squares[...] = jnp.zeros_like(squares)
    reduce_begin(1)

    reduce_hop(0)
    arrive(("next", 0), got2[0].at[dp, z])
    own_to_z("b", 0, got2[0])
    own_to_x("b", 0, got2[0])
    dpre_t[...] = dot(jnp.where(eye(F, F), 1.0, 0.0).astype(BF16), dpre_s[...], NT).astype(BF16)
    lax.fori_loop(0, 8, weight_grad_chunk, 0)
    for g in range(GROUPS):
        gather_end("a", g, got1[g])
    arrive(("next", 1), got2[1].at[dp, z])
    own_to_x("b", 1, got2[1])
    reduce_hop(1)
    for g in range(GROUPS):
        predecessor(g)
    sums_x()
    events = gather_events(
        "b",
        got2,
        {(0, 1): [(reduce_z, 0)], (1, 0): [(reduce_z, 1)], (1, 4): [(sums_core,)]},
    )
    steps(second_layer(0), events[0])
    finish_second(0)
    steps(second_layer(1), events[1])
    finish_second(1)

    active = as_column(preempted_v[...].astype(F32)) * jnp.where(section < sections - 1, 1.0, 0.0)
    arrive(("S", "c"), s_cr)
    sums = (s_c[...] + s_cr[...])[:, :T] / features
    mean_grad = as_column(sums[0:1])
    mean_proj = as_column(sums[1:2])
    inv_std = inv_s[:, 0:1]
    x_hat = (act_v[0].astype(F32) - mean_s[:, 0:1]) * inv_std
    held[...] = grad_v[0].astype(F32) - inv_std * (mean_grad + x_hat * mean_proj)
    hat_s[...] = x_hat
    gain_grad = jnp.zeros((1, F), F32)
    for g in range(GROUPS):
        dnormed = reduce_end(g)
        gain_grad = gain_grad + jnp.sum(dnormed * hat_s[rows[g]], axis=0, keepdims=True)
        dhat = dnormed * gain_v[...].astype(F32)
        rows_out[2, rows[g]] = (held[rows[g]] + inv_s[rows[g], 0:1] * dhat).astype(BF16)
    gain_grad_out[...] = gain_grad

    for k in (1, 2, 3):
        sent(("S", "z", k), s_own)
        sent(("S", "x", k), s_x)
    sent(("S", "c"), s_c)
    for g in range(GROUPS):
        gather_end("b", g, got2[g])
        sent(("back", g), outgoing[g])
        for k in (1, 2, 3):
            sent(("Z", g, k), h_out[g].at[k - 1])
        for n in range(4):
            sent(("C", g, n), partial[g].at[0])
        for j in range(2):
            sent(("F", g, j), hop[g].at[0])
            for part in range(2):
                sent(("G", g, j, part), hop[g].at[0])

    for g in range(GROUPS):
        arrive(("back", g), returned[g])
        shadow = unpack(returned[g][: count[g]].astype(F32), returned[g][count[g] :].astype(F32), odd)
        rows_out[1, rows[g]] = (shadow * active[rows[g]]).astype(BF16)


def shards(sections, act_in, grad_in, weight, gain, preempted):
    _, T, F = act_in.shape
    D = weight.shape[2]
    C = 4 * F
    anywhere = pl.BlockSpec(memory_space=pl.ANY)
    shape = jax.ShapeDtypeStruct
    copies = len(COPIES)
    count = (SPLIT[0], T - SPLIT[0])
    folded = [n + n // 2 for n in count]
    results = (
        shape((3, T, F), BF16),
        shape((1, F), F32),
        shape((1, F, D), BF16),
    )

    def blocks(*lead, extra=(0, 0)):
        return tuple(pltpu.VMEM((*lead, m + e, LANES), BF16) for m, e in zip(folded, extra))

    results = pl.pallas_call(
        functools.partial(kernel, sections, float(D)),
        out_shape=results,
        in_specs=[anywhere] * 5,
        out_specs=(pl.BlockSpec(memory_space=pltpu.VMEM),) * 3,
        scratch_shapes=[
            pltpu.VMEM((1, T, F), BF16),
            pltpu.VMEM((1, T, F), BF16),
            pltpu.VMEM((1, F), BF16),
            pltpu.VMEM((1, T), jnp.int32),
            pltpu.VMEM((8, F, C), BF16),
            pltpu.VMEM((8, F + PAD, C), BF16),
            pltpu.VMEM((8, PAD + T, C), BF16),
            pltpu.VMEM((max(count), C), BF16),
            pltpu.VMEM((8, 8, C), F32),
            blocks(8, 4, extra=(PAD, 0)),
            blocks(8, 4),
            pltpu.VMEM((PAD + T, F + PAD), F32),
            pltpu.VMEM((T, LANES), F32),
            blocks(),
            blocks(),
            blocks(8, 4),
            blocks(4, 4),
            blocks(2, 2),
            blocks(2, 4),
            blocks(3),
            blocks(3),
            pltpu.VMEM((8, 256), F32),
            pltpu.VMEM((3, 8, 256), F32),
            pltpu.VMEM((8, 256), F32),
            pltpu.VMEM((3, 8, 256), F32),
            pltpu.VMEM((8, 256), F32),
            pltpu.VMEM((8, 256), F32),
            pltpu.VMEM((8, F), F32),
            pltpu.VMEM((T, LANES), F32),
            pltpu.VMEM((T, LANES), F32),
            pltpu.VMEM((T, F), BF16),
            pltpu.VMEM((F, T), BF16),
            pltpu.VMEM((T, F), F32),
            pltpu.VMEM((T, F), F32),
            pltpu.SemaphoreType.DMA((copies,)),
            pltpu.SemaphoreType.DMA((copies,)),
            pltpu.SemaphoreType.DMA((8,)),
            pltpu.SemaphoreType.DMA((4,)),
        ],
        compiler_params=pltpu.CompilerParams(
            collective_id=0, has_side_effects=True, vmem_limit_bytes=48 * 1024 * 1024
        ),
    )(*[pltpu.with_memory_space_constraint(a, pltpu.HBM) for a in (act_in, grad_in, gain, preempted, weight)])
    by_row, gain_grad, weight_grad = results
    next_input, shadow, input_grad = by_row[0:1], by_row[1:2], by_row[2:3]
    return next_input, shadow, input_grad, weight_grad, gain_grad


def solution(mesh):
    return jax.shard_map(
        functools.partial(shards, mesh.shape["section"]),
        mesh=mesh,
        in_specs=(
            P("section", None, ("dp", "mp")),
            P("section", None, ("dp", "mp")),
            P("section", ("dp", "mp"), None),
            P("section", ("dp", "mp")),
            P("section", None),
        ),
        out_specs=(
            P("section", None, ("dp", "mp")),
            P("section", None, ("dp", "mp")),
            P("section", None, ("dp", "mp")),
            P("section", ("dp", "mp"), None),
            P("section", ("dp", "mp")),
        ),
        check_vma=False,
    )
```
